256 devices in a mesh: dp: 4 (over z_lo), ctx: 64 (over y, x, z_hi, core).
Axes of the slice: x: 4, y: 4, z: 8 (z_hi: 2, z_lo: 4; z = z_hi * 4 + z_lo), core: 2. Of those that a mesh axis runs over, the one named last changes fastest.
Arguments:
- queries: bfloat16 [4, 64, 128, 1024], P('dp', 'ctx'), may hold values from -256 to 256
- keys: bfloat16 [4, 64, 128, 1024], P('dp', 'ctx'), may hold values from -6 to 6
- values: bfloat16 [4, 64, 128, 1024], P('dp', 'ctx'), may hold values from -6 to 6
- d_out: bfloat16 [4, 64, 128, 1024], P('dp', 'ctx'), may hold values from -6 to 6
- out_weight: bfloat16 [1024, 1024], P('ctx'), may hold values from -0.1875 to 0.1875
- bar_lengths: int32 [4, 64], P('dp'), may hold values from 1 to 128, as said below
- summary_pos: int32 [4, 64], P('dp'), may hold values from 0 to 127, as said below
Outputs:
- d_queries: bfloat16 [4, 64, 128, 1024], P('dp', 'ctx')
- d_keys: bfloat16 [4, 64, 128, 1024], P('dp', 'ctx')
- d_values: bfloat16 [4, 64, 128, 1024], P('dp', 'ctx')
- d_weight: float32 [1024, 1024], P('ctx')
The draws below stay inside these ranges and needn't reach their ends.
Inputs may be any that keep to these rules, and one draw needn't show every extreme that they name: `bar_lengths`: the first bar of each score is full (128) and the second holds one token. summary_pos of a bar is below that bar's length.
All inputs are finite; a program needn't handle non-finite values.
Results may differ from the reference program's by a relative error of at most 0.0062.
Values may be sent and summed in bfloat16 or wider, within the bound.
A program may use at most 64 MiB of HBM per device.

```python
import jax
import jax.numpy as jnp
from jax import lax

D = 1024
HEADS = 16
HEAD = 64
BAR = 128
BARS_DEV = 1
BARS = 64
SCORES = 4


def shared_keys(key):
    key = jax.random.fold_in(key, 101)
    return jnp.clip(jax.random.normal(key, (SCORES, BARS, BAR, D), jnp.float32), -6.0, 6.0)


def bar_sizes(key):
    key = jax.random.fold_in(key, 202)
    lengths = jax.random.randint(key, (SCORES, BARS), 1, BAR + 1, jnp.int32)
    return lengths.at[:, 0].set(BAR).at[:, 1].set(1)


def draw_keys(key, part):
    base = shared_keys(key)
    return base.astype(jnp.bfloat16)


def draw_queries(key, part):
    key = jax.random.fold_in(key, 2)
    fresh = jnp.clip(jax.random.normal(key, (SCORES, BARS, BAR, D), jnp.float32), -6.0, 6.0)
    return fresh.astype(jnp.bfloat16)


def draw_bar_lengths(key, part):
    return bar_sizes(key)


def draw_summary_pos(key, part):
    lengths = bar_sizes(key)
    key = jax.random.fold_in(key, 3)
    spots = jax.random.randint(key, (SCORES, BARS), 0, lengths, jnp.int32)
    return spots.at[:, 0].set(BAR - 1).astype(jnp.int32)


def level_of(key, dims, pieces, low, largest):
    gain, own = 1.0, jax.random.fold_in(key, 6)
    for axis_at, parts in pieces:
        draws = jnp.exp(jax.random.uniform(jax.random.fold_in(own, axis_at), (parts,), jnp.float32, low / len(pieces), largest / len(pieces)))
        gain = gain * jnp.repeat(draws, dims[axis_at] // parts).reshape([-1 if axis == axis_at else 1 for axis in range(len(dims))])
    return gain


def scatter_about(own_key, dims, scale, most, split=(), kind=jnp.bfloat16):
    drawn = scale * jax.random.normal(own_key, dims, jnp.float32)
    if split:
        drawn = drawn * level_of(own_key, dims, split, -0.22, 0.18)
    return jnp.clip(drawn, -most, most).astype(kind)


def setup_inputs(seed: int = 0) -> dict:
    arg_keys = jax.random.split(jax.random.key(seed), 8)
    return {
        "queries": draw_queries(jax.random.fold_in(arg_keys[7], 71), 0),
        "keys": draw_keys(jax.random.fold_in(arg_keys[7], 71), 0),
        "values": scatter_about(arg_keys[2], (SCORES, BARS, BAR, D), 1.0, 6.0, ((0, 4), (1, 64))),
        "d_out": scatter_about(arg_keys[3], (SCORES, BARS, BAR, D), 1.0, 6.0, ((0, 4), (1, 64))),
        "out_weight": scatter_about(arg_keys[4], (D, D), D ** -0.5, 0.1875, ((0, 64),)),
        "bar_lengths": draw_bar_lengths(jax.random.fold_in(arg_keys[7], 71), 0),
        "summary_pos": draw_summary_pos(jax.random.fold_in(arg_keys[7], 71), 0),
    }


structure_offsets = (1, 2, 4, 8, 12, 16, 24, 32)


def shift_bars(block, offset):
    count = block.shape[0]
    if offset >= count:
        return jnp.zeros_like(block)
    filler = jnp.zeros((offset,) + block.shape[1:], block.dtype)
    return jnp.concatenate([filler, block[:count - offset]], axis=0)


def back_bars(block, offset):
    count = block.shape[0]
    if offset >= count:
        return jnp.zeros_like(block)
    filler = jnp.zeros((offset,) + block.shape[1:], block.dtype)
    return jnp.concatenate([block[offset:], filler], axis=0)


def route_terms(fine, bar_ids, per_dev):
    local = fine[:, 0]
    partial_sums = {}
    for index, offset in enumerate(structure_offsets):
        moved = back_bars(fine[:, 1 + index], offset)
        distance = (bar_ids + offset) // per_dev - bar_ids // per_dev
        for step in sorted({(r + offset) // per_dev for r in range(per_dev)}):
            piece = jnp.where((distance == step)[:, None, None], moved, jnp.float32(0.0))
            if step == 0:
                local = local + piece
            else:
                partial_sums[step] = partial_sums.get(step, jnp.zeros_like(local)) + piece
    total = local
    for step in sorted(partial_sums):
        rounded = lax.optimization_barrier(partial_sums[step].astype(jnp.bfloat16))
        total = total + rounded.astype(jnp.float32)
    return total


def head_grads(q_head, k_head, v_head, g_head, lengths, spos):
    nbars, bar, head = q_head.shape
    scale = head ** -0.5
    bar_ids = jnp.arange(nbars, dtype=jnp.int32)
    tpos = jnp.arange(bar, dtype=jnp.int32)
    own_mask = (tpos[None, :, None] >= tpos[None, None, :]) & (tpos[None, None, :] < lengths[:, None, None])
    masks = [own_mask]
    k_parts = [k_head]
    v_parts = [v_head]
    for offset in structure_offsets:
        source = bar_ids - offset
        source_len = jnp.where(source >= 0, lengths[jnp.clip(source, 0, nbars - 1)], 0)
        valid = (tpos[None, :] < source_len[:, None])[:, None, :]
        masks.append(jnp.broadcast_to(valid, (nbars, bar, bar)))
        k_parts.append(shift_bars(k_head, offset))
        v_parts.append(shift_bars(v_head, offset))
    summary_mask = jnp.broadcast_to((bar_ids[None, :] < bar_ids[:, None])[:, None, :], (nbars, bar, nbars))
    mask = jnp.concatenate(masks + [summary_mask], axis=2)
    k_all = jnp.concatenate(k_parts, axis=1).astype(jnp.float32)
    v_all = jnp.concatenate(v_parts, axis=1).astype(jnp.float32)
    nfine = k_all.shape[1]
    sum_k = k_head[bar_ids, spos].astype(jnp.float32)
    sum_v = v_head[bar_ids, spos].astype(jnp.float32)
    q_f = q_head.astype(jnp.float32)
    g_f = g_head.astype(jnp.float32)
    s_fine = jnp.einsum('bte,bse->bts', q_f, k_all) * scale
    s_sum = jnp.einsum('bte,ce->btc', q_f, sum_k) * scale
    scores = jnp.where(mask, jnp.concatenate([s_fine, s_sum], axis=2), -jnp.inf)
    top = jnp.max(scores, axis=2, keepdims=True)
    expo = jnp.exp(scores - top)
    probs = expo / jnp.sum(expo, axis=2, keepdims=True)
    pb = lax.optimization_barrier(probs.astype(jnp.bfloat16)).astype(jnp.float32)
    p_fine = pb[:, :, :nfine]
    p_sum = pb[:, :, nfine:]
    attn = jnp.einsum('bts,bse->bte', p_fine, v_all) + jnp.einsum('btc,ce->bte', p_sum, sum_v)
    delta = jnp.sum(g_f * attn, axis=2, keepdims=True)
    dprob = jnp.concatenate([jnp.einsum('bte,bse->bts', g_f, v_all), jnp.einsum('bte,ce->btc', g_f, sum_v)], axis=2)
    ds = lax.optimization_barrier((probs * (dprob - delta)).astype(jnp.bfloat16)).astype(jnp.float32)
    ds_fine = ds[:, :, :nfine]
    ds_sum = ds[:, :, nfine:]
    d_q = (jnp.einsum('bts,bse->bte', ds_fine, k_all) + jnp.einsum('btc,ce->bte', ds_sum, sum_k)) * scale
    dk_fine = (jnp.einsum('bts,bte->bse', ds_fine, q_f) * scale).reshape(nbars, nfine // bar, bar, head)
    dv_fine = jnp.einsum('bts,bte->bse', p_fine, g_f).reshape(nbars, nfine // bar, bar, head)
    dk_sum = jnp.einsum('btc,bte->ce', ds_sum, q_f) * scale
    dv_sum = jnp.einsum('btc,bte->ce', p_sum, g_f)
    d_k = route_terms(dk_fine, bar_ids, BARS_DEV).at[bar_ids, spos].add(dk_sum)
    d_v = route_terms(dv_fine, bar_ids, BARS_DEV).at[bar_ids, spos].add(dv_sum)
    return d_q.astype(jnp.bfloat16), d_k.astype(jnp.bfloat16), d_v.astype(jnp.bfloat16), attn.astype(jnp.bfloat16)


def join_heads(stacked):
    moved = jnp.moveaxis(stacked, 0, -2)
    return moved.reshape(moved.shape[:-2] + (-1,))


def score_grads(items, out_weight):
    queries, keys, values, d_out, lengths, spos = items
    nbars, bar, width = queries.shape
    flat_g = d_out.reshape(nbars * bar, width)
    d_attn = jnp.dot(flat_g, out_weight.T, preferred_element_type=jnp.float32).astype(jnp.bfloat16)
    d_attn = d_attn.reshape(nbars, bar, width)

    def one_head(index):
        def cut(block):
            return lax.dynamic_slice_in_dim(block, index * HEAD, HEAD, 2)
        return head_grads(cut(queries), cut(keys), cut(values), cut(d_attn), lengths, spos)

    d_q, d_k, d_v, attn = lax.map(one_head, jnp.arange(HEADS, dtype=jnp.int32))
    attn_flat = join_heads(attn).reshape(nbars * bar, width)
    d_weight = lax.dot_general(attn_flat, flat_g, (((0,), (0,)), ((), ())), preferred_element_type=jnp.float32)
    return join_heads(d_q), join_heads(d_k), join_heads(d_v), d_weight


def reference(queries, keys, values, d_out, out_weight, bar_lengths, summary_pos):
    d_q, d_k, d_v, d_weight = lax.map(lambda items: score_grads(items, out_weight),
                                      (queries, keys, values, d_out, bar_lengths, summary_pos))
    return d_q, d_k, d_v, jnp.sum(d_weight, axis=0)
```

```python
import jax
import jax.numpy as jnp
from jax import lax
from jax.experimental import pallas as pl
from jax.experimental.pallas import tpu as pltpu
from jax.sharding import PartitionSpec as P

N = 16
BAR = 128
HEAD = 64
WIDTH = 1024
PAD = 8
NKEYS = 1280
OWN_STEPS = (1, 2, 3, 4, 6, 8)
LOW = -1e30
MESH = pl.DeviceIdType.MESH
BF = jnp.bfloat16
F32 = jnp.float32


def remote(src, dst, send, recv, device):
    return pltpu.make_async_remote_copy(
        src_ref=src, dst_ref=dst, send_sem=send, recv_sem=recv, device_id=device, device_id_type=MESH
    )


def loop(low, high, body):
    def step(i, carry):
        body(i)
        return carry

    lax.fori_loop(low, high, step, 0)


def dot_nt(a, b):
    return lax.dot_general(a, b, (((1,), (1,)), ((), ())), preferred_element_type=F32)


def dot(a, b):
    return jnp.dot(a, b, preferred_element_type=F32)


def kernel(
    q_ref, k_ref, v_ref, do_ref, w_ref, len_ref, spot_ref,
    dq_ref, dk_ref, dv_ref, dw_ref,
    kvs, kvo, p1, p2, kvot, p1t, p2t, qgs, qgr, w4, do2, sumf, sumkv, sumt,
    b_ref, s_ref, x_ref, cat, catt, acc, accsum, d1s, d1r, d2s, d2r, d2f, sgr,
    fks, fkr, dqs, dqr, ats, atr, dws, dwr, wsum, zs, zr,
    kv_s, kv_r, p1_s, p1_r, p2_s, p2_r, wa_s, wa_r, wb_s, wb_r, wc_s, wc_r, do_s, do_r,
    qg_s, qg_r, sm_s, sm_r, d1_s, d1_rs, d2_s, d2_rs, sg_s, sg_rs, fk_s, fk_rs,
    dq_s, dq_rs, at_s, at_rs, dw_s, dw_rs, z_s, z_rs,
):
    dp = lax.axis_index("dp")
    ctx = lax.axis_index("ctx")
    i0 = lax.div(ctx, 4)
    r = lax.rem(ctx, 4)
    zh = lax.div(r, 2)
    core = lax.rem(r, 2)
    z = zh * 4 + dp
    odd = core == 1
    even = core == 0
    me = (dp, ctx)
    sib = (dp, 4 * i0 + 2 * zh + (1 - core))
    far = (dp, 4 * i0 + 2 * (1 - zh) + core)
    diag = (dp, 4 * i0 + 2 * (1 - zh) + (1 - core))

    def peer(j):
        return (dp, 4 * j + r)

    def near(j, c):
        return (dp, 4 * j + 2 * zh + c)

    def zpeer(t):
        return (lax.rem(t, 4), 4 * i0 + 2 * lax.div(t, 4) + core)

    def rot(d):
        return lax.rem(i0 + d, N)

    barrier = pltpu.get_barrier_semaphore()

    def greet(device):
        pl.semaphore_signal(barrier, inc=1, device_id=device, device_id_type=MESH)

    loop(0, N, lambda d: greet(near(rot(d), 1 - core)))
    loop(1, N, lambda d: greet(peer(rot(d))))
    loop(1, 8, lambda d: greet(zpeer(lax.rem(z + d, 8))))
    greet(diag)

    for p in range(N // 2):
        cols = slice(128 * p, 128 * p + 128)
        kk = k_ref[:, cols]
        vv = v_ref[:, cols]
        kvs[2 * p] = jnp.concatenate([kk[:, :HEAD], vv[:, :HEAD]], axis=1)
        kvs[2 * p + 1] = jnp.concatenate([kk[:, HEAD:], vv[:, HEAD:]], axis=1)
    zero = jnp.zeros((BAR, BAR), BF)
    for n in range(PAD):
        kvo[n] = zero
        kvot[n] = zero
    p1[0] = zero
    p1t[0] = zero
    p2[0] = zero
    p2t[0] = zero
    cat[pl.ds(1152, 128), :] = zero
    catt[:, pl.ds(1152, 128)] = zero
    x_ref[pl.ds(1152, 128), :] = jnp.zeros((128, 256), BF)
    acc[...] = jnp.zeros(acc.shape, F32)
    accsum[...] = jnp.zeros(accsum.shape, F32)
    kvo[PAD + i0] = kvs[i0]
    w4[i0, zh, core] = w_ref[...]
    do2[core] = do_ref[...]

    pl.semaphore_wait(barrier, 39)

    wa = remote(w4.at[i0, zh, core], w4.at[i0, zh, core], wa_s.at[0], wa_r.at[0], far)
    wa.start()

    def send_kv(d):
        j = rot(d)
        remote(kvs.at[j], kvo.at[PAD + i0], kv_s.at[j], kv_r.at[i0], peer(j)).start()

    loop(1, N, send_kv)
    do_copy = remote(do2.at[core], do2.at[core], do_s.at[0], do_r.at[0], sib)
    do_copy.start()
    remote(w4.at[i0, 1 - zh, core], w4.at[i0, 1 - zh, core], wa_s.at[0], wa_r.at[0], far).wait_recv()

    def send_w(d):
        j = rot(d)
        remote(w4.at[i0, :, core], w4.at[i0, :, core], wb_s.at[j], wb_r.at[i0], peer(j)).start()

    loop(1, N, send_w)

    row = lax.broadcasted_iota(jnp.int32, (BAR, BAR), 0)
    col = lax.broadcasted_iota(jnp.int32, (BAR, BAR), 1)

    def pass_on(j):
        @pl.when(j != i0)
        def _():
            remote(kvs.at[j], kvo.at[PAD + j], kv_s.at[j], kv_r.at[j], peer(j)).wait_recv()

        remote(kvo.at[PAD + j], p2.at[1 + j], p2_s.at[j], p2_r.at[j], far).start()

        @pl.when(even)
        def _():
            remote(kvo.at[PAD + j], p1.at[1 + j], p1_s.at[j], p1_r.at[j], sib).start()

        block = kvo[PAD + j]
        kvot[PAD + j] = block.T
        spot = spot_ref[0, 4 * j + r]
        picked = jnp.where(row == spot, block.astype(F32), 0.0)
        sumf[pl.ds(j, 1), :] = jnp.sum(picked, axis=0, keepdims=True)

    loop(0, N, pass_on)
    sumkv[r] = sumf[...].astype(BF)
    r_sib = 2 * zh + (1 - core)
    r_far = 2 * (1 - zh) + core
    r_diag = 2 * (1 - zh) + (1 - core)
    others = ((sib, r_sib), (far, r_far), (diag, r_diag))
    for device, rr in others:
        remote(sumkv.at[r], sumkv.at[r], sm_s.at[rr], sm_r.at[r], device).start()

    def pass_w(d):
        j = rot(d)

        @pl.when(d > 0)
        def _():
            remote(w4.at[j, :, core], w4.at[j, :, core], wb_s.at[j], wb_r.at[j], peer(j)).wait_recv()

        remote(w4.at[j, :, core], w4.at[j, :, core], wc_s.at[j], wc_r.at[j], sib).start()

    loop(0, N, pass_w)

    for c in range(4):
        for j in range(4 * c, 4 * c + 4):
            remote(w4.at[j, :, 1 - core], w4.at[j, :, 1 - core], wc_s.at[j], wc_r.at[j], sib).wait_recv()
        rows = w4[4 * c : 4 * c + 4].reshape(256, WIDTH)
        g = dot_nt(do_ref[...], rows).astype(BF)
        qq = (q_ref[:, 256 * c : 256 * c + 256].astype(F32) * 0.125).astype(BF)
        for h in range(4):
            cols = slice(HEAD * h, HEAD * h + HEAD)
            qgs[4 * c + h] = jnp.concatenate([qq[:, cols], g[:, cols]], axis=1)
        for h in range(4 * c, 4 * c + 4):
            @pl.when(i0 != h)
            def _():
                remote(qgs.at[h], qgr.at[i0], qg_s.at[h], qg_r.at[i0], peer(h)).start()

    qgr[i0] = qgs[i0]

    for device, rr in others:
        remote(sumkv.at[rr], sumkv.at[rr], sm_s.at[rr], sm_r.at[rr], device).wait_recv()
    cat[pl.ds(1152, 64), :] = sumkv[...].reshape(64, BAR)
    catt[:, pl.ds(1152, 128)] = cat[pl.ds(1152, 128), :].T

    lag1 = jnp.where(r < 1, 1, 0)
    lag2 = jnp.where(r < 2, 1, 0)
    srow = lax.broadcasted_iota(jnp.int32, (64, BAR), 0)
    sbar = 4 * lax.rem(srow, 16) + lax.div(srow, 16)
    left = col < HEAD

    def join(i):
        @pl.when(odd)
        def _():
            remote(d1s.at[i], d1r.at[i], d1_s.at[i], d1_rs.at[i], sib).wait_recv()
            d2s[i] = (d2f[lax.rem(i, 2)] + d1r[i].astype(F32)).astype(BF)
            remote(d2s.at[i], d2r.at[i], d2_s.at[i], d2_rs.at[i], far).start()

    def one_bar(i):
        bar = 4 * i + r

        @pl.when(i != i0)
        def _():
            remote(qgs.at[i], qgr.at[i], qg_s.at[i], qg_r.at[i], peer(i)).wait_recv()

        remote(kvo.at[PAD + i], p2.at[1 + i], p2_s.at[i], p2_r.at[i], far).wait_recv()

        @pl.when(odd)
        def _():
            remote(p2.at[1 + i], p1.at[1 + i], p1_s.at[i], p1_r.at[i], sib).start()

        remote(kvo.at[PAD + i], p1.at[1 + i], p1_s.at[i], p1_r.at[i], sib).wait_recv()
        p1t[1 + i] = p1[1 + i].T
        p2t[1 + i] = p2[1 + i].T

        blocks = [(kvo, kvot, PAD + i, 0), (p1, p1t, 1 + i - lag1, 1), (p2, p2t, 1 + i - lag2, 2)]
        blocks += [(kvo, kvot, PAD + i - m, 4 * m) for m in OWN_STEPS]
        lens = []
        for n, (src, srct, at, offset) in enumerate(blocks):
            cat[pl.ds(128 * n, 128), :] = src[at]
            catt[:, pl.ds(128 * n, 128)] = srct[at]
            source = bar - offset
            length = len_ref[0, jnp.maximum(source, 0)]
            lens.append(jnp.where(source >= 0, length, 0))

        qg = qgr[i]
        none = jnp.zeros_like(qg)
        b_ref[pl.ds(0, 128), :] = jnp.where(left, qg, none)
        b_ref[pl.ds(128, 128), :] = jnp.where(left, none, qg)
        s_ref[...] = dot_nt(cat[...], b_ref[...])

        spans = [(128 * n, 128) for n in range(9)] + [(1152, 64)]
        top = jnp.full((8, BAR), LOW, F32)
        for n, (at, size) in enumerate(spans):
            s = s_ref[pl.ds(at, size), 0:128]
            if n == 0:
                keep = (row <= col) & (row < lens[0])
            elif n < 9:
                keep = row < lens[n]
            else:
                keep = sbar < bar
            s = jnp.where(keep, s, LOW)
            s_ref[pl.ds(at, size), 0:128] = s
            top = jnp.maximum(top, jnp.max(s.reshape(size // 8, 8, BAR), axis=0))
        top = jnp.max(top, axis=0, keepdims=True)
        total = jnp.zeros((8, BAR), F32)
        for at, size in spans:
            e = jnp.exp(s_ref[pl.ds(at, size), 0:128] - top)
            s_ref[pl.ds(at, size), 0:128] = e
            total = total + jnp.sum(e.reshape(size // 8, 8, BAR), axis=0)
        inv = 1.0 / jnp.sum(total, axis=0, keepdims=True)
        delta = jnp.zeros((8, BAR), F32)
        for at, size in spans:
            prob = s_ref[pl.ds(at, size), 0:128] * inv
            pb = prob.astype(BF)
            x_ref[pl.ds(at, size), 128:256] = pb
            term = pb.astype(F32) * s_ref[pl.ds(at, size), 128:256]
            delta = delta + jnp.sum(term.reshape(size // 8, 8, BAR), axis=0)
        delta = jnp.sum(delta, axis=0, keepdims=True)
        for at, size in spans:
            prob = s_ref[pl.ds(at, size), 0:128] * inv
            ds = prob * (s_ref[pl.ds(at, size), 128:256] - delta)
            x_ref[pl.ds(at, size), 0:128] = ds.astype(BF)

        out = dot(catt[...], x_ref[...])
        dqs[i] = (out[0:HEAD, 0:128] * 0.125).astype(BF)
        ats[i] = out[HEAD:128, 128:256].astype(BF)

        half = lax.div(i0, 8)
        slot = lax.rem(i0, 8)

        @pl.when(i != i0)
        def _():
            remote(dqs.at[i], dqr.at[i0], dq_s.at[i], dq_rs.at[i0], peer(i)).start()

        @pl.when(i == i0)
        def _():
            dqr[i] = dqs[i]

        here = jnp.logical_and(i == i0, core == half)

        @pl.when(jnp.logical_not(here))
        def _():
            remote(ats.at[i], atr.at[core, slot], at_s.at[i], at_rs.at[core, slot], near(i, half)).start()

        @pl.when(here)
        def _():
            atr[core, slot] = ats[i]

        rhs = b_ref[...]
        for n, (src, _, at, offset) in enumerate(blocks):
            term = dot(x_ref[pl.ds(128 * n, 128), :], rhs)
            if n == 1:
                d1s[i] = term.astype(BF)
                remote(d1s.at[i], d1r.at[i], d1_s.at[i], d1_rs.at[i], sib).start()
            elif n == 2:
                d2f[lax.rem(i, 2)] = term

                @pl.when(even)
                def _():
                    d2s[i] = term.astype(BF)
                    remote(d2s.at[i], d2r.at[i], d2_s.at[i], d2_rs.at[i], far).start()
            else:
                acc[at] += term
        accsum[...] += dot(x_ref[pl.ds(1152, 64), :], rhs).reshape(4, 16, BAR)

        @pl.when(i > 0)
        def _():
            join(i - 1)

    loop(0, N, one_bar)

    for device, rr in others:
        remote(accsum.at[rr], sgr.at[r], sg_s.at[rr], sg_rs.at[r], device).start()
    join(N - 1)

    remote(do2.at[1 - core], do2.at[1 - core], do_s.at[0], do_r.at[0], sib).wait_recv()

    def get_attn(h):
        head = 8 * core + h
        for c in range(2):
            @pl.when(jnp.logical_not(jnp.logical_and(head == i0, core == c)))
            def _():
                remote(ats.at[0], atr.at[c, h], at_s.at[0], at_rs.at[c, h], sib).wait_recv()

    loop(0, 8, get_attn)

    def project(t):
        lhs = jnp.concatenate(
            [atr[0, pl.ds(2 * t, 2)].reshape(128, BAR), atr[1, pl.ds(2 * t, 2)].reshape(128, BAR)], axis=1
        )
        part = dot(lhs, do2[...].reshape(256, WIDTH)).astype(BF)
        dws[pl.ds(2 * t, 2)] = part.reshape(2, 2, 2, 16, WIDTH)
        for u in range(2):
            h = 2 * t + u
            head = 8 * core + h
            remote(
                dws.at[h, :, 1 - core], dwr.at[i0], dw_s.at[h, 1 - core], dw_rs.at[i0], near(head, 1 - core)
            ).start()

            @pl.when(head != i0)
            def _():
                remote(dws.at[h, :, core], dwr.at[i0], dw_s.at[h, core], dw_rs.at[i0], peer(head)).start()

            @pl.when(head == i0)
            def _():
                dwr[i0] = dws[h, :, core]

    loop(0, 4, project)

    for device, rr in others:
        remote(accsum.at[rr], sgr.at[rr], sg_s.at[rr], sg_rs.at[rr], device).wait_recv()
    sgr[r] = accsum[r]
    sumf[...] = sgr[0] + sgr[1] + sgr[2] + sgr[3]
    back = jnp.where(r >= 2, 1, 0)

    def gather_terms(i):
        remote(d2s.at[i], d2r.at[i], d2_s.at[i], d2_rs.at[i], far).wait_recv()
        acc[PAD + i - back] += d2r[i].astype(F32)

        @pl.when(even)
        def _():
            remote(d1s.at[i], d1r.at[i], d1_s.at[i], d1_rs.at[i], sib).wait_recv()
            acc[PAD + i] += d1r[i].astype(F32)

    loop(0, N, gather_terms)

    def finish(d):
        j = rot(d)
        spot = spot_ref[0, 4 * j + r]
        extra = jnp.where(row == spot, sumf[pl.ds(j, 1), :], 0.0)
        fks[j] = (acc[PAD + j] + extra).astype(BF)

        @pl.when(d > 0)
        def _():
            remote(fks.at[j], fkr.at[i0], fk_s.at[j], fk_rs.at[i0], peer(j)).start()

    loop(0, N, finish)
    fkr[i0] = fks[i0]

    def get_dw(j):
        @pl.when(jnp.logical_not(jnp.logical_and(j == i0, core == lax.div(i0, 8))))
        def _():
            remote(dws.at[0, :, 0], dwr.at[j], dw_s.at[0, 0], dw_rs.at[j], sib).wait_recv()

    loop(0, N, get_dw)
    for a in range(2):
        part = dwr[0, a].astype(F32)
        for j in range(1, N):
            part = part + dwr[j, a].astype(F32)
        wsum[a] = part
        zs[a] = part.astype(BF)

    def send_z(d):
        t = lax.rem(z + d, 8)
        remote(zs.at[lax.div(t, 4)], zr.at[z], z_s.at[t], z_rs.at[z], zpeer(t)).start()

    loop(1, 8, send_z)

    def get_dq(d):
        j = rot(d)
        remote(dqs.at[j], dqr.at[j], dq_s.at[j], dq_rs.at[j], peer(j)).wait_recv()

    loop(1, N, get_dq)
    for p in range(N // 2):
        dq_ref[:, 128 * p : 128 * p + 128] = dqr[2 * p : 2 * p + 2].reshape(128, 128).T

    def get_fk(d):
        j = rot(d)
        remote(fks.at[j], fkr.at[j], fk_s.at[j], fk_rs.at[j], peer(j)).wait_recv()

    loop(1, N, get_fk)
    for p in range(N // 2):
        cols = slice(128 * p, 128 * p + 128)
        a = fkr[2 * p]
        b = fkr[2 * p + 1]
        dk_ref[:, cols] = jnp.concatenate([a[:, :HEAD], b[:, :HEAD]], axis=1)
        dv_ref[:, cols] = jnp.concatenate([a[:, HEAD:], b[:, HEAD:]], axis=1)

    def get_z(d):
        t = lax.rem(z + d, 8)
        remote(zs.at[0], zr.at[t], z_s.at[t], z_rs.at[t], zpeer(t)).wait_recv()

    loop(1, 8, get_z)
    zr[z] = zs[zh]
    whole = wsum[zh]

    def add_z(d, total):
        return total + zr[lax.rem(z + d, 8)].astype(F32)

    dw_ref[...] = lax.fori_loop(1, 8, add_z, whole)

    wa.wait_send()
    do_copy.wait_send()

    def drain(d):
        j = rot(d)
        remote(kvs.at[j], kvo.at[PAD + i0], kv_s.at[j], kv_r.at[i0], peer(j)).wait_send()
        remote(w4.at[i0, :, core], w4.at[i0, :, core], wb_s.at[j], wb_r.at[i0], peer(j)).wait_send()
        remote(qgs.at[j], qgr.at[i0], qg_s.at[j], qg_r.at[i0], peer(j)).wait_send()
        remote(dqs.at[j], dqr.at[i0], dq_s.at[j], dq_rs.at[i0], peer(j)).wait_send()
        remote(fks.at[j], fkr.at[i0], fk_s.at[j], fk_rs.at[i0], peer(j)).wait_send()

    loop(1, N, drain)

    def drain_all(j):
        remote(kvo.at[PAD + j], p2.at[1 + j], p2_s.at[j], p2_r.at[j], far).wait_send()
        remote(kvo.at[PAD + j], p1.at[1 + j], p1_s.at[j], p1_r.at[j], sib).wait_send()
        remote(w4.at[j, :, core], w4.at[j, :, core], wc_s.at[j], wc_r.at[j], sib).wait_send()
        remote(d1s.at[j], d1r.at[j], d1_s.at[j], d1_rs.at[j], sib).wait_send()
        remote(d2s.at[j], d2r.at[j], d2_s.at[j], d2_rs.at[j], far).wait_send()

        @pl.when(jnp.logical_not(jnp.logical_and(j == i0, core == lax.div(i0, 8))))
        def _():
            remote(ats.at[j], atr.at[0, 0], at_s.at[j], at_rs.at[0, 0], sib).wait_send()

    loop(0, N, drain_all)

    def drain_w(h):
        head = 8 * core + h
        remote(dws.at[h, :, 1 - core], dwr.at[i0], dw_s.at[h, 1 - core], dw_rs.at[i0], sib).wait_send()

        @pl.when(head != i0)
        def _():
            remote(dws.at[h, :, core], dwr.at[i0], dw_s.at[h, core], dw_rs.at[i0], peer(head)).wait_send()

    loop(0, 8, drain_w)

    def drain_z(d):
        t = lax.rem(z + d, 8)
        remote(zs.at[lax.div(t, 4)], zr.at[z], z_s.at[t], z_rs.at[z], zpeer(t)).wait_send()

    loop(1, 8, drain_z)
    for device, rr in others:
        remote(sumkv.at[r], sumkv.at[r], sm_s.at[rr], sm_r.at[r], device).wait_send()
        remote(accsum.at[rr], sgr.at[r], sg_s.at[rr], sg_rs.at[r], device).wait_send()


def on_device(queries, keys, values, d_out, out_weight, bar_lengths, summary_pos):
    vm = pltpu.VMEM
    dma = pltpu.SemaphoreType.DMA
    blocks = lambda n, kind=BF: vm((n, BAR, BAR), kind)
    scratch = [
        blocks(N), blocks(PAD + N), blocks(1 + N), blocks(1 + N),
        blocks(PAD + N), blocks(1 + N), blocks(1 + N),
        blocks(N), blocks(N),
        vm((N, 2, 2, 16, WIDTH), BF), vm((2, BAR, WIDTH), BF),
        vm((16, BAR), F32), vm((4, 16, BAR), BF), vm((BAR, BAR), BF),
        vm((256, BAR), BF), vm((NKEYS, 256), F32), vm((NKEYS, 256), BF),
        vm((NKEYS, BAR), BF), vm((BAR, NKEYS), BF),
        blocks(PAD + N, F32), vm((4, 16, BAR), F32),
        blocks(N), blocks(N), blocks(N), blocks(N), blocks(2, F32), vm((4, 16, BAR), F32),
        blocks(N), blocks(N),
        vm((N, HEAD, BAR), BF), vm((N, HEAD, BAR), BF),
        vm((N, HEAD, BAR), BF), vm((2, 8, HEAD, BAR), BF),
        vm((8, 2, 2, 16, WIDTH), BF), vm((N, 2, 16, WIDTH), BF),
        vm((2, 16, WIDTH), F32), vm((2, 16, WIDTH), BF), vm((8, 16, WIDTH), BF),
    ]
    sems = [(N,)] * 6 + [(1,)] * 2 + [(N,)] * 4 + [(1,)] * 2 + [(N,)] * 2 + [(4,)] * 2
    sems += [(N,)] * 4 + [(4,)] * 2 + [(N,)] * 4 + [(N,), (2, 8), (8, 2), (N,), (8,), (8,)]
    scratch += [dma(shape) for shape in sems]
    in_vmem = pl.BlockSpec(memory_space=pltpu.VMEM)
    in_smem = pl.BlockSpec(memory_space=pltpu.SMEM)
    rows = jax.ShapeDtypeStruct((BAR, WIDTH), BF)
    d_q, d_k, d_v, d_w = pl.pallas_call(
        kernel,
        out_shape=(rows, rows, rows, jax.ShapeDtypeStruct((16, WIDTH), F32)),
        in_specs=[in_vmem] * 5 + [in_smem] * 2,
        out_specs=(in_vmem,) * 4,
        scratch_shapes=scratch,
        compiler_params=pltpu.CompilerParams(
            collective_id=0, has_side_effects=True, vmem_limit_bytes=48 * 1024 * 1024
        ),
    )(queries[0, 0], keys[0, 0], values[0, 0], d_out[0, 0], out_weight, bar_lengths, summary_pos)
    return d_q[None, None], d_k[None, None], d_v[None, None], d_w


def solution(mesh):
    spread = P("dp", "ctx", None, None)
    return jax.shard_map(
        on_device,
        mesh=mesh,
        in_specs=(spread,) * 4 + (P("ctx", None), P("dp", None), P("dp", None)),
        out_specs=(spread,) * 3 + (P("ctx", None),),
        check_vma=False,
    )
```

```python
import jax
import jax.numpy as jnp
from jax import lax
from jax.experimental import pallas as pl
from jax.experimental.pallas import tpu as pltpu
from jax.sharding import PartitionSpec as P

N = 16
BAR = 128
HEAD = 64
WIDTH = 1024
PAD = 8
NKEYS = 1280
OWN_STEPS = (1, 2, 3, 4, 6, 8)
AHEAD = 6
LAG_J = 2
LAG = 6
LAG_P = 4
LAG_W = 8
LOW = -1e30
MESH = pl.DeviceIdType.MESH
BF = jnp.bfloat16
F32 = jnp.float32


def remote(src, dst, send, recv, device):
    return pltpu.make_async_remote_copy(
        src_ref=src, dst_ref=dst, send_sem=send, recv_sem=recv, device_id=device, device_id_type=MESH
    )


def loop(low, high, body):
    def step(i, carry):
        body(i)
        return carry

    lax.fori_loop(low, high, step, 0)


def dot_nt(a, b):
    return lax.dot_general(a, b, (((1,), (1,)), ((), ())), preferred_element_type=F32)


def dot(a, b):
    return jnp.dot(a, b, preferred_element_type=F32)


def kernel(
    q_hbm, k_hbm, v_hbm, do_hbm, w_hbm, len_ref, spot_ref,
    dq_ref, dk_ref, dv_ref, dw_ref,
    q_ref, k_ref, v_ref, kvs, kvo, p1, p2, kvot, p1t, p2t, qgs, qgr, w4, do2, sumf, sumkv, sumt,
    b_ref, s_ref, x_ref, cat, catt, acc, accsum, d1s, d1r, d2s, d2r, d2f, sgr,
    fks, fkr, dqs, dqr, ats, atr, dws, dwr, wsum, zs, zr,
    in_s, kv_s, kv_r, p1_s, p1_r, p2_s, p2_r, wa_s, wa_r, wb_s, wb_r, wc_s, wc_r, do_s, do_r,
    qg_s, qg_r, sm_s, sm_r, d1_s, d1_rs, d2_s, d2_rs, sg_s, sg_rs, fk_s, fk_rs,
    dq_s, dq_rs, at_s, at_rs, dw_s, dw_rs, z_s, z_rs,
):
    dp = lax.axis_index("dp")
    ctx = lax.axis_index("ctx")
    i0 = lax.div(ctx, 4)
    r = lax.rem(ctx, 4)
    zh = lax.div(r, 2)
    core = lax.rem(r, 2)
    z = zh * 4 + dp
    odd = core == 1
    even = core == 0
    me = (dp, ctx)
    sib = (dp, 4 * i0 + 2 * zh + (1 - core))
    far = (dp, 4 * i0 + 2 * (1 - zh) + core)
    diag = (dp, 4 * i0 + 2 * (1 - zh) + (1 - core))

    def peer(j):
        return (dp, 4 * j + r)

    def near(j, c):
        return (dp, 4 * j + 2 * zh + c)

    def zpeer(t):
        return (lax.rem(t, 4), 4 * i0 + 2 * lax.div(t, 4) + core)

    def rot(d):
        return lax.rem(i0 + d, N)

    loads = [
        pltpu.make_async_copy(k_hbm, k_ref, in_s.at[0]),
        pltpu.make_async_copy(v_hbm, v_ref, in_s.at[1]),
        pltpu.make_async_copy(w_hbm, w4.at[i0, zh, core], in_s.at[2]),
        pltpu.make_async_copy(do_hbm, do2.at[core], in_s.at[3]),
        pltpu.make_async_copy(q_hbm, q_ref, in_s.at[4]),
    ]
    for load in loads:
        load.start()

    barrier = pltpu.get_barrier_semaphore()

    def greet(device):
        pl.semaphore_signal(barrier, inc=1, device_id=device, device_id_type=MESH)

    loop(0, N, lambda d: greet(near(rot(d), 1 - core)))
    loop(1, N, lambda d: greet(peer(rot(d))))
    loop(1, 8, lambda d: greet(zpeer(lax.rem(z + d, 8))))
    greet(diag)

    loads[0].wait()
    loads[1].wait()
    for p in range(N // 2):
        cols = slice(128 * p, 128 * p + 128)
        kk = k_ref[:, cols]
        vv = v_ref[:, cols]
        kvs[2 * p] = jnp.concatenate([kk[:, :HEAD], vv[:, :HEAD]], axis=1)
        kvs[2 * p + 1] = jnp.concatenate([kk[:, HEAD:], vv[:, HEAD:]], axis=1)
    kvo[PAD + i0] = kvs[i0]
    loads[2].wait()
    loads[3].wait()
    loads[4].wait()
    pl.semaphore_wait(barrier, 39)

    wa = remote(w4.at[i0, zh, core], w4.at[i0, zh, core], wa_s.at[0], wa_r.at[0], far)
    wa.start()

    def send_kv(d):
        j = rot(d)
        remote(kvs.at[j], kvo.at[PAD + i0], kv_s.at[j], kv_r.at[i0], peer(j)).start()

    loop(1, N, send_kv)
    do_copy = remote(do2.at[core], do2.at[core], do_s.at[0], do_r.at[0], sib)
    do_copy.start()
    remote(w4.at[i0, 1 - zh, core], w4.at[i0, 1 - zh, core], wa_s.at[0], wa_r.at[0], far).wait_recv()

    def send_w(d):
        j = rot(d)
        remote(w4.at[i0, :, core], w4.at[i0, :, core], wb_s.at[j], wb_r.at[i0], peer(j)).start()

    loop(1, N, send_w)

    zero = jnp.zeros((BAR, BAR), BF)
    for n in range(PAD):
        kvo[n] = zero
        kvot[n] = zero
    p1[0] = zero
    p1t[0] = zero
    p2[0] = zero
    p2t[0] = zero
    cat[pl.ds(0, 128), :] = zero
    x_ref[pl.ds(0, 128), :] = jnp.zeros((128, 256), BF)
    acc[...] = jnp.zeros(acc.shape, F32)
    accsum[...] = jnp.zeros(accsum.shape, F32)
    wsum[...] = jnp.zeros(wsum.shape, F32)

    row = lax.broadcasted_iota(jnp.int32, (BAR, BAR), 0)
    col = lax.broadcasted_iota(jnp.int32, (BAR, BAR), 1)

    def pass_on(d):
        j = lax.rem(i0 - d + N, N)

        @pl.when(d > 0)
        def _():
            remote(kvs.at[j], kvo.at[PAD + j], kv_s.at[j], kv_r.at[j], peer(j)).wait_recv()

        remote(kvo.at[PAD + j], p2.at[1 + j], p2_s.at[j], p2_r.at[j], far).start()

        @pl.when(even)
        def _():
            remote(kvo.at[PAD + j], p1.at[1 + j], p1_s.at[j], p1_r.at[j], sib).start()

        block = kvo[PAD + j]
        kvot[PAD + j] = block.T
        spot = spot_ref[0, 4 * j + r]
        picked = jnp.where(row == spot, block.astype(F32), 0.0)
        sumf[pl.ds(j, 1), :] = jnp.sum(picked, axis=0, keepdims=True)

    loop(0, N, pass_on)
    sumkv[r] = sumf[...].astype(BF)
    r_sib = 2 * zh + (1 - core)
    r_far = 2 * (1 - zh) + core
    r_diag = 2 * (1 - zh) + (1 - core)
    others = ((sib, r_sib), (far, r_far), (diag, r_diag))
    for device, rr in others:
        remote(sumkv.at[r], sumkv.at[r], sm_s.at[rr], sm_r.at[r], device).start()

    def pass_w(d):
        j = rot(d)

        @pl.when(d > 0)
        def _():
            remote(w4.at[j, :, core], w4.at[j, :, core], wb_s.at[j], wb_r.at[j], peer(j)).wait_recv()

        remote(w4.at[j, :, core], w4.at[j, :, core], wc_s.at[j], wc_r.at[j], sib).start()

    loop(0, N, pass_w)

    for c in range(4):
        line = lax.rem(lax.div(i0, 4) + c, 4)
        for n in range(4):
            j = 4 * line + n
            remote(w4.at[j, :, 1 - core], w4.at[j, :, 1 - core], wc_s.at[j], wc_r.at[j], sib).wait_recv()
        rows = w4[pl.ds(4 * line, 4)].reshape(256, WIDTH)
        g = dot_nt(do2[core], rows).astype(BF)
        qq = q_ref[:, pl.ds(pl.multiple_of(256 * line, 256), 256)]
        qq = (qq.astype(F32) * 0.125).astype(BF)
        for n in range(4):
            cols = slice(HEAD * n, HEAD * n + HEAD)
            qgs[4 * line + n] = jnp.concatenate([qq[:, cols], g[:, cols]], axis=1)
        for n in range(4):
            h = 4 * line + lax.rem(i0 + n, 4)

            @pl.when(i0 != h)
            def _():
                remote(qgs.at[h], qgr.at[i0], qg_s.at[h], qg_r.at[i0], peer(h)).start()

    qgr[i0] = qgs[i0]

    for device, rr in others:
        remote(sumkv.at[rr], sumkv.at[rr], sm_s.at[rr], sm_r.at[rr], device).wait_recv()
    cat[pl.ds(0, 64), :] = sumkv[...].reshape(64, BAR)
    catt[:, pl.ds(0, 128)] = cat[pl.ds(0, 128), :].T

    def behind(t):
        return lax.rem(i0 - t + N, N)

    def take_far(t):
        j = behind(t)
        remote(kvo.at[PAD + j], p2.at[1 + j], p2_s.at[j], p2_r.at[j], far).wait_recv()

        @pl.when(odd)
        def _():
            remote(p2.at[1 + j], p1.at[1 + j], p1_s.at[j], p1_r.at[j], sib).start()

        p2t[1 + j] = p2[1 + j].T

    def take_near(t):
        j = behind(t)
        remote(kvo.at[PAD + j], p1.at[1 + j], p1_s.at[j], p1_r.at[j], sib).wait_recv()
        p1t[1 + j] = p1[1 + j].T

    loop(0, AHEAD, take_far)
    loop(0, AHEAD - 2, take_near)

    lag1 = jnp.where(r < 1, 1, 0)
    lag2 = jnp.where(r < 2, 1, 0)
    srow = lax.broadcasted_iota(jnp.int32, (64, BAR), 0)
    sbar = 4 * lax.rem(srow, 16) + lax.div(srow, 16)
    left = col < HEAD

    half = lax.rem(i0, 2)
    slot = lax.div(i0, 2)

    def send_far(i):
        @pl.when(jnp.logical_or(zh == 1, i > 0))
        def _():
            remote(d2s.at[i], d2r.at[i], d2_s.at[i], d2_rs.at[i], far).start()

    def join(i):
        @pl.when(odd)
        def _():
            remote(d1s.at[i], d1r.at[i], d1_s.at[i], d1_rs.at[i], sib).wait_recv()
            d2s[i] = (d2f[lax.rem(i, 4)] + d1r[i].astype(F32)).astype(BF)
            send_far(i)

    def take_terms(t):
        at = behind(t)

        @pl.when(jnp.logical_or(zh == 0, at > 0))
        def _():
            remote(d2s.at[at], d2r.at[at], d2_s.at[at], d2_rs.at[at], far).wait_recv()
            acc[PAD + at - zh] += d2r[at].astype(F32)

        @pl.when(even)
        def _():
            remote(d1s.at[at], d1r.at[at], d1_s.at[at], d1_rs.at[at], sib).wait_recv()
            acc[PAD + at] += d1r[at].astype(F32)

    def project(t):
        head = rot(t)

        @pl.when(lax.rem(head, 2) == core)
        def _():
            at = lax.div(head, 2)
            for c in range(2):
                @pl.when(jnp.logical_not(jnp.logical_and(t == 0, core == c)))
                def _():
                    remote(ats.at[0], atr.at[c, at], at_s.at[0], at_rs.at[c, at], sib).wait_recv()

            lhs = jnp.concatenate([atr[0, at], atr[1, at]], axis=1)
            part = dot(lhs, do2[...].reshape(256, WIDTH)).astype(BF)
            dws[at] = part.reshape(2, 2, 16, WIDTH)
            remote(
                dws.at[at, :, 1 - core], dwr.at[i0], dw_s.at[at, 1 - core], dw_rs.at[i0], near(head, 1 - core)
            ).start()

            @pl.when(t > 0)
            def _():
                remote(dws.at[at, :, core], dwr.at[i0], dw_s.at[at, core], dw_rs.at[i0], peer(head)).start()

            @pl.when(t == 0)
            def _():
                dwr[i0] = dws[at, :, core]

    def take_dw(t):
        j = behind(t)

        @pl.when(jnp.logical_not(jnp.logical_and(t == 0, core == half)))
        def _():
            remote(dws.at[0, :, 0], dwr.at[j], dw_s.at[0, 0], dw_rs.at[j], sib).wait_recv()

        wsum[...] += dwr[j].astype(F32)

    remote(do2.at[1 - core], do2.at[1 - core], do_s.at[0], do_r.at[0], sib).wait_recv()

    def attend(i, steps):
        bar = 4 * i + r
        blocks = [(kvo, kvot, PAD + i, 0), (p1, p1t, 1 + i - lag1, 1), (p2, p2t, 1 + i - lag2, 2)]
        blocks += [(kvo, kvot, PAD + i - m, 4 * m) for m in steps]
        lens = []
        for n, (src, srct, at, offset) in enumerate(blocks):
            cat[pl.ds(128 * n + 128, 128), :] = src[at]
            catt[:, pl.ds(128 * n + 128, 128)] = srct[at]
            source = bar - offset
            length = len_ref[0, jnp.maximum(source, 0)]
            lens.append(jnp.where(source >= 0, length, 0))

        qg = qgr[i]
        none = jnp.zeros_like(qg)
        b_ref[pl.ds(0, 128), :] = jnp.where(left, qg, none)
        b_ref[pl.ds(128, 128), :] = jnp.where(left, none, qg)
        size_all = 128 * len(blocks) + 128
        s_ref[pl.ds(0, size_all), :] = dot_nt(cat[pl.ds(0, size_all), :], b_ref[...])

        spans = [(128 * n + 128, 128) for n in range(len(blocks))] + [(0, 64)]
        top = jnp.full((8, BAR), LOW, F32)
        for n, (at, size) in enumerate(spans):
            s = s_ref[pl.ds(at, size), 0:128]
            if n == 0:
                keep = (row <= col) & (row < lens[0])
            elif n < len(blocks):
                keep = row < lens[n]
            else:
                keep = sbar < bar
            s = jnp.where(keep, s, LOW)
            s_ref[pl.ds(at, size), 0:128] = s
            top = jnp.maximum(top, jnp.max(s.reshape(size // 8, 8, BAR), axis=0))
        top = jnp.max(top, axis=0, keepdims=True)
        total = jnp.zeros((8, BAR), F32)
        for at, size in spans:
            e = jnp.exp(s_ref[pl.ds(at, size), 0:128] - top)
            s_ref[pl.ds(at, size), 0:128] = e
            total = total + jnp.sum(e.reshape(size // 8, 8, BAR), axis=0)
        inv = 1.0 / jnp.sum(total, axis=0, keepdims=True)
        delta = jnp.zeros((8, BAR), F32)
        for at, size in spans:
            prob = s_ref[pl.ds(at, size), 0:128] * inv
            pb = prob.astype(BF)
            x_ref[pl.ds(at, size), 128:256] = pb
            term = pb.astype(F32) * s_ref[pl.ds(at, size), 128:256]
            delta = delta + jnp.sum(term.reshape(size // 8, 8, BAR), axis=0)
        delta = jnp.sum(delta, axis=0, keepdims=True)
        for at, size in spans:
            prob = s_ref[pl.ds(at, size), 0:128] * inv
            ds = prob * (s_ref[pl.ds(at, size), 128:256] - delta)
            x_ref[pl.ds(at, size), 0:128] = ds.astype(BF)

        out = dot(catt[:, pl.ds(0, size_all)], x_ref[pl.ds(0, size_all), :])
        dqs[i] = (out[0:HEAD, 0:128] * 0.125).astype(BF)
        ats[i] = out[HEAD:128, 128:256].astype(BF)

        rhs = b_ref[...]
        for n, (src, _, at, offset) in enumerate(blocks):
            term = dot(x_ref[pl.ds(128 * n + 128, 128), :], rhs)
            if n == 1:
                d1s[i] = term.astype(BF)
                remote(d1s.at[i], d1r.at[i], d1_s.at[i], d1_rs.at[i], sib).start()
            elif n == 2:
                d2f[lax.rem(i, 4)] = term

                @pl.when(even)
                def _():
                    d2s[i] = term.astype(BF)
                    send_far(i)
            else:
                acc[at] += term
        accsum[...] += dot(x_ref[pl.ds(0, 64), :], rhs)

    def one_bar(t):
        i = behind(t)

        @pl.when(t + AHEAD < N)
        def _():
            take_far(t + AHEAD)

        @pl.when(t + AHEAD - 2 < N)
        def _():
            take_near(t + AHEAD - 2)

        @pl.when(i != i0)
        def _():
            remote(qgs.at[i], qgr.at[i], qg_s.at[i], qg_r.at[i], peer(i)).wait_recv()


        @pl.when(i >= 8)
        def _():
            attend(i, OWN_STEPS)

        @pl.when(jnp.logical_and(i >= 4, i < 8))
        def _():
            attend(i, OWN_STEPS[:5])

        @pl.when(i < 4)
        def _():
            attend(i, OWN_STEPS[:3])

        @pl.when(i != i0)
        def _():
            remote(dqs.at[i], dqr.at[i0], dq_s.at[i], dq_rs.at[i0], peer(i)).start()

        @pl.when(i == i0)
        def _():
            dqr[i] = dqs[i]

        here = jnp.logical_and(i == i0, core == half)

        @pl.when(jnp.logical_not(here))
        def _():
            remote(ats.at[i], atr.at[core, slot], at_s.at[i], at_rs.at[core, slot], near(i, half)).start()

        @pl.when(here)
        def _():
            atr[core, slot] = ats[i]

        @pl.when(t >= LAG_J)
        def _():
            join(behind(t - LAG_J))

        @pl.when(t >= LAG_P)
        def _():
            project(t - LAG_P)

        @pl.when(t >= LAG)
        def _():
            take_terms(t - LAG)

        @pl.when(t >= LAG_W)
        def _():
            take_dw(t - LAG_W)

    loop(0, N, one_bar)
    loop(N - LAG_J, N, lambda t: join(behind(t)))
    for device, rr in others:
        remote(accsum.at[pl.ds(16 * rr, 16)], sgr.at[r], sg_s.at[rr], sg_rs.at[r], device).start()
    loop(N - LAG_P, N, project)
    loop(N - LAG, N, take_terms)

    for device, rr in others:
        remote(sgr.at[rr], sgr.at[rr], sg_s.at[rr], sg_rs.at[rr], device).wait_recv()
    sgr[r] = accsum[pl.ds(16 * r, 16), :]
    sumf[...] = sgr[0] + sgr[1] + sgr[2] + sgr[3]

    def finish(d):
        j = rot(d)
        spot = spot_ref[0, 4 * j + r]
        extra = jnp.where(row == spot, sumf[pl.ds(j, 1), :], 0.0)
        fks[j] = (acc[PAD + j] + extra).astype(BF)

        @pl.when(d > 0)
        def _():
            remote(fks.at[j], fkr.at[i0], fk_s.at[j], fk_rs.at[i0], peer(j)).start()

    loop(0, N, finish)
    fkr[i0] = fks[i0]

    loop(N - LAG_W, N, take_dw)
    zs[...] = wsum[...].astype(BF)

    def send_z(d):
        t = lax.rem(z + d, 8)
        remote(zs.at[lax.div(t, 4)], zr.at[z], z_s.at[t], z_rs.at[z], zpeer(t)).start()

    loop(1, 8, send_z)

    def get_dq(d):
        j = rot(d)
        remote(dqs.at[j], dqr.at[j], dq_s.at[j], dq_rs.at[j], peer(j)).wait_recv()

    loop(1, N, get_dq)
    for p in range(N // 2):
        dq_ref[:, 128 * p : 128 * p + 128] = dqr[2 * p : 2 * p + 2].reshape(128, 128).T

    def get_fk(d):
        j = rot(d)
        remote(fks.at[j], fkr.at[j], fk_s.at[j], fk_rs.at[j], peer(j)).wait_recv()

    loop(1, N, get_fk)
    for p in range(N // 2):
        cols = slice(128 * p, 128 * p + 128)
        a = fkr[2 * p]
        b = fkr[2 * p + 1]
        dk_ref[:, cols] = jnp.concatenate([a[:, :HEAD], b[:, :HEAD]], axis=1)
        dv_ref[:, cols] = jnp.concatenate([a[:, HEAD:], b[:, HEAD:]], axis=1)

    def get_z(d):
        t = lax.rem(z + d, 8)
        remote(zs.at[0], zr.at[t], z_s.at[t], z_rs.at[t], zpeer(t)).wait_recv()

    loop(1, 8, get_z)
    zr[z] = zs[zh]
    whole = wsum[zh]

    def add_z(d, total):
        return total + zr[lax.rem(z + d, 8)].astype(F32)

    dw_ref[...] = lax.fori_loop(1, 8, add_z, whole)

    wa.wait_send()
    do_copy.wait_send()

    def drain(d):
        j = rot(d)
        remote(kvs.at[j], kvo.at[PAD + i0], kv_s.at[j], kv_r.at[i0], peer(j)).wait_send()
        remote(w4.at[i0, :, core], w4.at[i0, :, core], wb_s.at[j], wb_r.at[i0], peer(j)).wait_send()
        remote(qgs.at[j], qgr.at[i0], qg_s.at[j], qg_r.at[i0], peer(j)).wait_send()
        remote(dqs.at[j], dqr.at[i0], dq_s.at[j], dq_rs.at[i0], peer(j)).wait_send()
        remote(fks.at[j], fkr.at[i0], fk_s.at[j], fk_rs.at[i0], peer(j)).wait_send()

    loop(1, N, drain)

    def drain_all(j):
        remote(kvo.at[PAD + j], p2.at[1 + j], p2_s.at[j], p2_r.at[j], far).wait_send()
        remote(kvo.at[PAD + j], p1.at[1 + j], p1_s.at[j], p1_r.at[j], sib).wait_send()
        remote(w4.at[j, :, core], w4.at[j, :, core], wc_s.at[j], wc_r.at[j], sib).wait_send()
        remote(d1s.at[j], d1r.at[j], d1_s.at[j], d1_rs.at[j], sib).wait_send()

        @pl.when(jnp.logical_or(zh == 1, j > 0))
        def _():
            remote(d2s.at[j], d2r.at[j], d2_s.at[j], d2_rs.at[j], far).wait_send()


        @pl.when(jnp.logical_not(jnp.logical_and(j == i0, core == half)))
        def _():
            remote(ats.at[j], atr.at[0, 0], at_s.at[j], at_rs.at[0, 0], sib).wait_send()

    loop(0, N, drain_all)

    def drain_w(h):
        head = 2 * h + core
        remote(dws.at[h, :, 1 - core], dwr.at[i0], dw_s.at[h, 1 - core], dw_rs.at[i0], sib).wait_send()

        @pl.when(head != i0)
        def _():
            remote(dws.at[h, :, core], dwr.at[i0], dw_s.at[h, core], dw_rs.at[i0], peer(head)).wait_send()

    loop(0, 8, drain_w)

    def drain_z(d):
        t = lax.rem(z + d, 8)
        remote(zs.at[lax.div(t, 4)], zr.at[z], z_s.at[t], z_rs.at[z], zpeer(t)).wait_send()

    loop(1, 8, drain_z)
    for device, rr in others:
        remote(sumkv.at[r], sumkv.at[r], sm_s.at[rr], sm_r.at[r], device).wait_send()
        remote(accsum.at[pl.ds(16 * rr, 16)], sgr.at[r], sg_s.at[rr], sg_rs.at[r], device).wait_send()


def on_device(queries, keys, values, d_out, out_weight, bar_lengths, summary_pos):
    vm = pltpu.VMEM
    dma = pltpu.SemaphoreType.DMA
    blocks = lambda n, kind=BF: vm((n, BAR, BAR), kind)
    flat = vm((BAR, WIDTH), BF)
    scratch = [
        flat, flat, flat, blocks(N), blocks(PAD + N), blocks(1 + N), blocks(1 + N),
        blocks(PAD + N), blocks(1 + N), blocks(1 + N),
        blocks(N), blocks(N),
        vm((N, 2, 2, 16, WIDTH), BF), vm((2, BAR, WIDTH), BF),
        vm((16, BAR), F32), vm((4, 16, BAR), BF), vm((BAR, BAR), BF),
        vm((256, BAR), BF), vm((NKEYS, 256), F32), vm((NKEYS, 256), BF),
        vm((NKEYS, BAR), BF), vm((BAR, NKEYS), BF),
        blocks(PAD + N, F32), vm((64, BAR), F32),
        blocks(N), blocks(N), blocks(N), blocks(N), blocks(4, F32), vm((4, 16, BAR), F32),
        blocks(N), blocks(N),
        vm((N, HEAD, BAR), BF), vm((N, HEAD, BAR), BF),
        vm((N, HEAD, BAR), BF), vm((2, 8, HEAD, BAR), BF),
        vm((8, 2, 2, 16, WIDTH), BF), vm((N, 2, 16, WIDTH), BF),
        vm((2, 16, WIDTH), F32), vm((2, 16, WIDTH), BF), vm((8, 16, WIDTH), BF),
    ]
    sems = [(5,)] + [(N,)] * 6 + [(1,)] * 2 + [(N,)] * 4 + [(1,)] * 2 + [(N,)] * 2 + [(4,)] * 2
    sems += [(N,)] * 4 + [(4,)] * 2 + [(N,)] * 4 + [(N,), (2, 8), (8, 2), (N,), (8,), (8,)]
    scratch += [dma(shape) for shape in sems]
    in_vmem = pl.BlockSpec(memory_space=pltpu.VMEM)
    in_smem = pl.BlockSpec(memory_space=pltpu.SMEM)
    rows = jax.ShapeDtypeStruct((BAR, WIDTH), BF)
    d_q, d_k, d_v, d_w = pl.pallas_call(
        kernel,
        out_shape=(rows, rows, rows, jax.ShapeDtypeStruct((16, WIDTH), F32)),
        in_specs=[pl.BlockSpec(memory_space=pltpu.HBM)] * 5 + [in_smem] * 2,
        out_specs=(in_vmem,) * 4,
        scratch_shapes=scratch,
        compiler_params=pltpu.CompilerParams(
            collective_id=0, has_side_effects=True, vmem_limit_bytes=48 * 1024 * 1024
        ),
    )(queries[0, 0], keys[0, 0], values[0, 0], d_out[0, 0], out_weight, bar_lengths, summary_pos)
    return d_q[None, None], d_k[None, None], d_v[None, None], d_w


def solution(mesh):
    spread = P("dp", "ctx", None, None)
    return jax.shard_map(
        on_device,
        mesh=mesh,
        in_specs=(spread,) * 4 + (P("ctx", None), P("dp", None), P("dp", None)),
        out_specs=(spread,) * 3 + (P("ctx", None),),
        check_vma=False,
    )
```

```python
import jax
import jax.numpy as jnp
from jax import lax
from jax.experimental import pallas as pl
from jax.experimental.pallas import tpu as pltpu
from jax.sharding import PartitionSpec as P

N = 16
BAR = 128
HEAD = 64
WIDTH = 1024
PAD = 8
NKEYS = 1280
OWN_STEPS = (1, 2, 3, 4, 6, 8)
BEHIND = 1
AHEAD = 6
LAG_J = 2
LAG = 6
LAG_P = 4
LAG_W = 8
LOW = -1e30
MESH = pl.DeviceIdType.MESH
BF = jnp.bfloat16
F32 = jnp.float32


def remote(src, dst, send, recv, device):
    return pltpu.make_async_remote_copy(
        src_ref=src, dst_ref=dst, send_sem=send, recv_sem=recv, device_id=device, device_id_type=MESH
    )


def loop(low, high, body):
    def step(i, carry):
        body(i)
        return carry

    lax.fori_loop(low, high, step, 0)


def dot_nt(a, b):
    return lax.dot_general(a, b, (((1,), (1,)), ((), ())), preferred_element_type=F32)


def dot(a, b):
    return jnp.dot(a, b, preferred_element_type=F32)


def kernel(
    q_hbm, k_hbm, v_hbm, do_hbm, w_hbm, len_ref, spot_ref,
    dq_ref, dk_ref, dv_ref, dw_ref,
    q_ref, k_ref, v_ref, kvs, kvo, p1, p2, kvot, p1t, p2t, qts, qtr, gts, gtr, w4, do2, sumf, sumkv, sumt,
    b_ref, s_ref, x_ref, pb_ref, ps, cat, catt, acc, accsum, d1s, d1r, d2s, d2r, d2f, sgr,
    fks, fkr, dqs, dqr, ats, atr, dws, dwr, wsum, zs, zr,
    in_s, kv_s, kv_r, p1_s, p1_r, p2_s, p2_r, wa_s, wa_r, wb_s, wb_r, wc_s, wc_r, do_s, do_r,
    qt_s, qt_r, gt_s, gt_r, sm_s, sm_r, d1_s, d1_rs, d2_s, d2_rs, sg_s, sg_rs, fk_s, fk_rs,
    dq_s, dq_rs, at_s, at_rs, dw_s, dw_rs, z_s, z_rs,
):
    dp = lax.axis_index("dp")
    ctx = lax.axis_index("ctx")
    i0 = lax.div(ctx, 4)
    r = lax.rem(ctx, 4)
    zh = lax.div(r, 2)
    core = lax.rem(r, 2)
    z = zh * 4 + dp
    odd = core == 1
    even = core == 0
    me = (dp, ctx)
    sib = (dp, 4 * i0 + 2 * zh + (1 - core))
    far = (dp, 4 * i0 + 2 * (1 - zh) + core)
    diag = (dp, 4 * i0 + 2 * (1 - zh) + (1 - core))

    def peer(j):
        return (dp, 4 * j + r)

    def near(j, c):
        return (dp, 4 * j + 2 * zh + c)

    def zpeer(t):
        return (lax.rem(t, 4), 4 * i0 + 2 * lax.div(t, 4) + core)

    def rot(d):
        return lax.rem(i0 + d, N)

    loads = [
        pltpu.make_async_copy(k_hbm, k_ref, in_s.at[0]),
        pltpu.make_async_copy(v_hbm, v_ref, in_s.at[1]),
        pltpu.make_async_copy(w_hbm, w4.at[i0, zh, core], in_s.at[2]),
        pltpu.make_async_copy(do_hbm, do2.at[core], in_s.at[3]),
        pltpu.make_async_copy(q_hbm, q_ref, in_s.at[4]),
    ]
    for load in loads:
        load.start()

    barrier = pltpu.get_barrier_semaphore()

    def greet(device):
        pl.semaphore_signal(barrier, inc=1, device_id=device, device_id_type=MESH)

    loop(0, N, lambda d: greet(near(rot(d), 1 - core)))
    loop(1, N, lambda d: greet(peer(rot(d))))
    loop(1, 8, lambda d: greet(zpeer(lax.rem(z + d, 8))))
    greet(diag)

    loads[0].wait()
    loads[1].wait()
    for p in range(N // 2):
        cols = slice(128 * p, 128 * p + 128)
        kk = k_ref[:, cols]
        vv = v_ref[:, cols]
        kvs[2 * p] = jnp.concatenate([kk[:, :HEAD], vv[:, :HEAD]], axis=1)
        kvs[2 * p + 1] = jnp.concatenate([kk[:, HEAD:], vv[:, HEAD:]], axis=1)
    kvo[PAD + i0] = kvs[i0]
    loads[2].wait()
    loads[3].wait()
    loads[4].wait()
    for p in range(N // 2):
        qq = (q_ref[:, 128 * p : 128 * p + 128].astype(F32) * 0.125).astype(BF)
        qts[pl.ds(2 * p, 2)] = qq.T.reshape(2, HEAD, BAR)
    qtr[i0] = qts[i0]
    zero = jnp.zeros((BAR, BAR), BF)
    for n in range(PAD):
        kvo[n] = zero
        kvot[n] = zero
    p1[0] = zero
    p1t[0] = zero
    p2[0] = zero
    p2t[0] = zero
    cat[pl.ds(0, 128), :] = zero
    x_ref[pl.ds(0, 128), :] = jnp.zeros((128, 256), BF)
    acc[...] = jnp.zeros(acc.shape, F32)
    accsum[...] = jnp.zeros(accsum.shape, F32)
    wsum[...] = jnp.zeros(wsum.shape, F32)
    pb_ref[pl.ds(0, 128), :] = zero
    pl.semaphore_wait(barrier, 39)

    wa = remote(w4.at[i0, zh, core], w4.at[i0, zh, core], wa_s.at[0], wa_r.at[0], far)
    wa.start()

    def send_kv(d):
        j = rot(d)
        remote(kvs.at[j], kvo.at[PAD + i0], kv_s.at[j], kv_r.at[i0], peer(j)).start()

    loop(1, N, send_kv)

    def send_q(d):
        j = rot(d)
        remote(qts.at[j], qtr.at[i0], qt_s.at[j], qt_r.at[i0], peer(j)).start()

    loop(1, N, send_q)
    do_copy = remote(do2.at[core], do2.at[core], do_s.at[0], do_r.at[0], sib)
    do_copy.start()
    remote(w4.at[i0, 1 - zh, core], w4.at[i0, 1 - zh, core], wa_s.at[0], wa_r.at[0], far).wait_recv()

    step_u = 1 + 3 * core
    step_v = 4 - 3 * core
    pos_u = lax.rem(lax.div(i0, step_u), 4)
    pos_v = lax.rem(lax.div(i0, step_v), 4)

    def cell(du, dv):
        return lax.rem(pos_u + du, 4) * step_u + lax.rem(pos_v + dv, 4) * step_v

    def send_w(j, to, key):
        at = w4.at[j, :, core]
        remote(at, at, wb_s.at[key], wb_r.at[j], peer(to)).start()

    for du in (1, 3, 2):
        send_w(i0, cell(du, 0), cell(du, 0))

    row = lax.broadcasted_iota(jnp.int32, (BAR, BAR), 0)
    col = lax.broadcasted_iota(jnp.int32, (BAR, BAR), 1)

    def pass_on(d):
        j = lax.rem(i0 - d + N, N)

        @pl.when(d > 0)
        def _():
            remote(kvs.at[j], kvo.at[PAD + j], kv_s.at[j], kv_r.at[j], peer(j)).wait_recv()

        remote(kvo.at[PAD + j], p2.at[1 + j], p2_s.at[j], p2_r.at[j], far).start()

        @pl.when(even)
        def _():
            remote(kvo.at[PAD + j], p1.at[1 + j], p1_s.at[j], p1_r.at[j], sib).start()

        block = kvo[PAD + j]
        kvot[PAD + j] = block.T
        spot = spot_ref[0, 4 * j + r]
        picked = jnp.where(row == spot, block.astype(F32), 0.0)
        sumf[pl.ds(j, 1), :] = jnp.sum(picked, axis=0, keepdims=True)

    loop(0, N, pass_on)
    for du in (0, 1, 3, 2):
        j = cell(du, 0)
        if du > 0:
            remote(w4.at[j, :, core], w4.at[j, :, core], wb_s.at[j], wb_r.at[j], peer(j)).wait_recv()
        for dv in (1, 3, 2):
            send_w(j, cell(0, dv), cell(du, dv))
        remote(w4.at[j, :, core], w4.at[j, :, core], wc_s.at[j], wc_r.at[j], sib).start()
    sumkv[r] = sumf[...].astype(BF)
    r_sib = 2 * zh + (1 - core)
    r_far = 2 * (1 - zh) + core
    r_diag = 2 * (1 - zh) + (1 - core)
    others = ((sib, r_sib), (far, r_far), (diag, r_diag))
    for device, rr in others:
        remote(sumkv.at[r], sumkv.at[r], sm_s.at[rr], sm_r.at[r], device).start()

    def pass_w(j, own):
        if not own:
            remote(w4.at[j, :, core], w4.at[j, :, core], wb_s.at[j], wb_r.at[j], peer(j)).wait_recv()
        remote(w4.at[j, :, core], w4.at[j, :, core], wc_s.at[j], wc_r.at[j], sib).start()

    for dv in (1, 3, 2):
        for du in (0, 1, 3, 2):
            pass_w(cell(du, dv), False)

    def project_back():
        for c in range(4):
            line = lax.rem(lax.div(i0, 4) + c, 4)
            for n in range(4):
                j = 4 * line + n
                remote(w4.at[j, :, 1 - core], w4.at[j, :, 1 - core], wc_s.at[j], wc_r.at[j], sib).wait_recv()
            rows = w4[pl.ds(4 * line, 4)].reshape(256, WIDTH)
            gts[pl.ds(4 * line, 4)] = dot_nt(rows, do2[core]).astype(BF).reshape(4, HEAD, BAR)
            for n in range(4):
                h = 4 * line + lax.rem(i0 + n, 4)

                @pl.when(i0 != h)
                def _():
                    remote(gts.at[h], gtr.at[i0], gt_s.at[h], gt_r.at[i0], peer(h)).start()

        gtr[i0] = gts[i0]

    project_back()

    for device, rr in others:
        remote(sumkv.at[rr], sumkv.at[rr], sm_s.at[rr], sm_r.at[rr], device).wait_recv()
    cat[pl.ds(0, 64), :] = sumkv[...].reshape(64, BAR)
    catt[:, pl.ds(0, 128)] = cat[pl.ds(0, 128), :].T

    def behind(t):
        return lax.rem(i0 - t + N, N)

    def take_far(t):
        j = behind(t)
        remote(kvo.at[PAD + j], p2.at[1 + j], p2_s.at[j], p2_r.at[j], far).wait_recv()

        @pl.when(odd)
        def _():
            remote(p2.at[1 + j], p1.at[1 + j], p1_s.at[j], p1_r.at[j], sib).start()

        p2t[1 + j] = p2[1 + j].T

    def take_near(t):
        j = behind(t)
        remote(kvo.at[PAD + j], p1.at[1 + j], p1_s.at[j], p1_r.at[j], sib).wait_recv()
        p1t[1 + j] = p1[1 + j].T

    loop(0, AHEAD, take_far)
    loop(0, AHEAD - 2, take_near)

    lag1 = jnp.where(r < 1, 1, 0)
    lag2 = jnp.where(r < 2, 1, 0)
    srow = lax.broadcasted_iota(jnp.int32, (64, BAR), 0)
    sbar = 4 * lax.rem(srow, 16) + lax.div(srow, 16)
    left = col < HEAD

    half = lax.rem(i0, 2)
    slot = lax.div(i0, 2)

    def send_far(i):
        @pl.when(jnp.logical_or(zh == 1, i > 0))
        def _():
            remote(d2s.at[i], d2r.at[i], d2_s.at[i], d2_rs.at[i], far).start()

    def join(i):
        @pl.when(odd)
        def _():
            remote(d1s.at[i], d1r.at[i], d1_s.at[i], d1_rs.at[i], sib).wait_recv()
            d2s[i] = (d2f[lax.rem(i, 4)] + d1r[i].astype(F32)).astype(BF)
            send_far(i)

    def take_terms(t):
        at = behind(t)

        @pl.when(jnp.logical_or(zh == 0, at > 0))
        def _():
            remote(d2s.at[at], d2r.at[at], d2_s.at[at], d2_rs.at[at], far).wait_recv()
            acc[PAD + at - zh] += d2r[at].astype(F32)

        @pl.when(even)
        def _():
            remote(d1s.at[at], d1r.at[at], d1_s.at[at], d1_rs.at[at], sib).wait_recv()
            acc[PAD + at] += d1r[at].astype(F32)

    def project(t):
        head = rot(t)

        @pl.when(lax.rem(head, 2) == core)
        def _():
            at = lax.div(head, 2)
            for c in range(2):
                @pl.when(jnp.logical_not(jnp.logical_and(t == 0, core == c)))
                def _():
                    remote(ats.at[0], atr.at[c, at], at_s.at[0], at_rs.at[c, at], sib).wait_recv()

            lhs = jnp.concatenate([atr[0, at], atr[1, at]], axis=1)
            part = dot(lhs, do2[...].reshape(256, WIDTH)).astype(BF)
            dws[at] = part.reshape(2, 2, 16, WIDTH)
            remote(
                dws.at[at, :, 1 - core], dwr.at[i0], dw_s.at[at, 1 - core], dw_rs.at[i0], near(head, 1 - core)
            ).start()

            @pl.when(t > 0)
            def _():
                remote(dws.at[at, :, core], dwr.at[i0], dw_s.at[at, core], dw_rs.at[i0], peer(head)).start()

            @pl.when(t == 0)
            def _():
                dwr[i0] = dws[at, :, core]

    def take_dw(t):
        j = behind(t)

        @pl.when(jnp.logical_not(jnp.logical_and(t == 0, core == half)))
        def _():
            remote(dws.at[0, :, 0], dwr.at[j], dw_s.at[0, 0], dw_rs.at[j], sib).wait_recv()

        wsum[...] += dwr[j].astype(F32)

    remote(do2.at[1 - core], do2.at[1 - core], do_s.at[0], do_r.at[0], sib).wait_recv()

    def gather(i, steps, lens=None):
        bar = 4 * i + r
        blocks = [(kvo, kvot, PAD + i, 0), (p1, p1t, 1 + i - lag1, 1), (p2, p2t, 1 + i - lag2, 2)]
        blocks += [(kvo, kvot, PAD + i - m, 4 * m) for m in steps]
        for n, (src, srct, at, offset) in enumerate(blocks):
            cat[pl.ds(128 * n + 128, 128), :] = src[at]
            catt[:, pl.ds(128 * n + 128, 128)] = srct[at]
            if lens is not None:
                source = bar - offset
                length = len_ref[0, jnp.maximum(source, 0)]
                lens.append(jnp.where(source >= 0, length, 0))
        spans = [(128 * n + 128, 128) for n in range(len(blocks))] + [(0, 64)]
        return blocks, spans, 128 * len(blocks) + 128

    nothing = jnp.zeros((HEAD, BAR), BF)

    def forward(i, steps):
        bar = 4 * i + r
        lens = []
        blocks, spans, size_all = gather(i, steps, lens)
        rhs = jnp.concatenate([qtr[i], nothing], axis=0)
        s_ref[pl.ds(0, size_all), :] = dot(cat[pl.ds(0, size_all), :], rhs)
        top = jnp.full((8, BAR), LOW, F32)
        for n, (at, size) in enumerate(spans):
            s = s_ref[pl.ds(at, size), :]
            if n == 0:
                keep = (row <= col) & (row < lens[0])
            elif n < len(blocks):
                keep = row < lens[n]
            else:
                keep = sbar < bar
            s = jnp.where(keep, s, LOW)
            s_ref[pl.ds(at, size), :] = s
            top = jnp.maximum(top, jnp.max(s.reshape(size // 8, 8, BAR), axis=0))
        top = jnp.max(top, axis=0, keepdims=True)
        total = jnp.zeros((8, BAR), F32)
        for at, size in spans:
            e = jnp.exp(s_ref[pl.ds(at, size), :] - top)
            s_ref[pl.ds(at, size), :] = e
            total = total + jnp.sum(e.reshape(size // 8, 8, BAR), axis=0)
        inv = 1.0 / jnp.sum(total, axis=0, keepdims=True)
        for at, size in spans:
            prob = s_ref[pl.ds(at, size), :] * inv
            ps[i, pl.ds(at, size), :] = prob
            pb_ref[pl.ds(at, size), :] = prob.astype(BF)
        out = dot(catt[HEAD:BAR, pl.ds(0, size_all)], pb_ref[pl.ds(0, size_all), :])
        ats[i] = out.astype(BF)

    def backward(i, steps):
        blocks, spans, size_all = gather(i, steps)
        rhs = jnp.concatenate([nothing, gtr[i]], axis=0)
        s_ref[pl.ds(0, size_all), :] = dot(cat[pl.ds(0, size_all), :], rhs)
        delta = jnp.zeros((8, BAR), F32)
        for at, size in spans:
            pb = ps[i, pl.ds(at, size), :].astype(BF)
            x_ref[pl.ds(at, size), 128:256] = pb
            term = pb.astype(F32) * s_ref[pl.ds(at, size), :]
            delta = delta + jnp.sum(term.reshape(size // 8, 8, BAR), axis=0)
        delta = jnp.sum(delta, axis=0, keepdims=True)
        for at, size in spans:
            ds = ps[i, pl.ds(at, size), :] * (s_ref[pl.ds(at, size), :] - delta)
            x_ref[pl.ds(at, size), 0:128] = ds.astype(BF)
        qg = jnp.concatenate([qtr[i], gtr[i]], axis=0).T
        none = jnp.zeros_like(qg)
        b_ref[pl.ds(0, 128), :] = jnp.where(left, qg, none)
        b_ref[pl.ds(128, 128), :] = jnp.where(left, none, qg)
        rhs = b_ref[...]
        for n in (1, 2, 0) + tuple(range(3, len(blocks))):
            term = dot(x_ref[pl.ds(128 * n + 128, 128), :], rhs)
            at = blocks[n][2]
            if n == 1:
                d1s[i] = term.astype(BF)
                remote(d1s.at[i], d1r.at[i], d1_s.at[i], d1_rs.at[i], sib).start()
            elif n == 2:
                d2f[lax.rem(i, 4)] = term

                @pl.when(even)
                def _():
                    d2s[i] = term.astype(BF)
                    send_far(i)
            else:
                acc[at] += term
        accsum[...] += dot(x_ref[pl.ds(0, 64), :], rhs)
        out = dot(catt[0:HEAD, pl.ds(0, size_all)], x_ref[pl.ds(0, size_all), 0:128])
        dqs[i] = (out * 0.125).astype(BF)

    def by_reach(i, work):
        @pl.when(i >= 8)
        def _():
            work(i, OWN_STEPS)

        @pl.when(jnp.logical_and(i >= 4, i < 8))
        def _():
            work(i, OWN_STEPS[:5])

        @pl.when(i < 4)
        def _():
            work(i, OWN_STEPS[:3])

    def first(t):
        i = behind(t)

        @pl.when(t + AHEAD < N)
        def _():
            take_far(t + AHEAD)

        @pl.when(t + AHEAD - 2 < N)
        def _():
            take_near(t + AHEAD - 2)

        @pl.when(i != i0)
        def _():
            remote(qts.at[i], qtr.at[i], qt_s.at[i], qt_r.at[i], peer(i)).wait_recv()

        by_reach(i, forward)
        here = jnp.logical_and(i == i0, core == half)

        @pl.when(jnp.logical_not(here))
        def _():
            remote(ats.at[i], atr.at[core, slot], at_s.at[i], at_rs.at[core, slot], near(i, half)).start()

        @pl.when(here)
        def _():
            atr[core, slot] = ats[i]

    def second(t):
        i = behind(t)

        @pl.when(i != i0)
        def _():
            remote(gts.at[i], gtr.at[i], gt_s.at[i], gt_r.at[i], peer(i)).wait_recv()

        by_reach(i, backward)

        @pl.when(i != i0)
        def _():
            remote(dqs.at[i], dqr.at[i0], dq_s.at[i], dq_rs.at[i0], peer(i)).start()

        @pl.when(i == i0)
        def _():
            dqr[i] = dqs[i]

    def send_z(d):
        t = lax.rem(z + d, 8)
        remote(zs.at[lax.div(t, 4)], zr.at[z], z_s.at[t], z_rs.at[z], zpeer(t)).start()

    def share_sum():
        zs[...] = wsum[...].astype(BF)
        loop(1, 8, send_z)

    def step(t):
        @pl.when(t < N)
        def _():
            first(t)

        @pl.when(jnp.logical_and(t >= LAG_P, t < N + LAG_P))
        def _():
            project(t - LAG_P)

        @pl.when(jnp.logical_and(t >= LAG_W, t < N + LAG_W))
        def _():
            take_dw(t - LAG_W)

        if LAG_W < BEHIND:
            @pl.when(t == N + LAG_W)
            def _():
                share_sum()

        @pl.when(t >= BEHIND)
        def _():
            second(t - BEHIND)

        @pl.when(t >= BEHIND + LAG_J)
        def _():
            join(behind(t - BEHIND - LAG_J))

        @pl.when(t >= BEHIND + LAG)
        def _():
            take_terms(t - BEHIND - LAG)

    loop(0, N + BEHIND, step)
    loop(N - LAG_J, N, lambda t: join(behind(t)))
    for device, rr in others:
        remote(accsum.at[pl.ds(16 * rr, 16)], sgr.at[r], sg_s.at[rr], sg_rs.at[r], device).start()
    loop(min(N, N + BEHIND - LAG_P), N, project)
    if LAG_W >= BEHIND:
        loop(N + BEHIND - LAG_W, N, take_dw)
        share_sum()
    loop(N - LAG, N, take_terms)

    for device, rr in others:
        remote(sgr.at[rr], sgr.at[rr], sg_s.at[rr], sg_rs.at[rr], device).wait_recv()
    sgr[r] = accsum[pl.ds(16 * r, 16), :]
    sumf[...] = sgr[0] + sgr[1] + sgr[2] + sgr[3]

    def finish(d):
        j = rot(d)
        spot = spot_ref[0, 4 * j + r]
        extra = jnp.where(row == spot, sumf[pl.ds(j, 1), :], 0.0)
        fks[j] = (acc[PAD + j] + extra).astype(BF)

        @pl.when(d > 0)
        def _():
            remote(fks.at[j], fkr.at[i0], fk_s.at[j], fk_rs.at[i0], peer(j)).start()

    loop(0, N, finish)
    fkr[i0] = fks[i0]

    def get_dq(d):
        j = rot(d)
        remote(dqs.at[j], dqr.at[j], dq_s.at[j], dq_rs.at[j], peer(j)).wait_recv()

    loop(1, N, get_dq)
    for p in range(N // 2):
        dq_ref[:, 128 * p : 128 * p + 128] = dqr[2 * p : 2 * p + 2].reshape(128, 128).T

    def get_fk(d):
        j = rot(d)
        remote(fks.at[j], fkr.at[j], fk_s.at[j], fk_rs.at[j], peer(j)).wait_recv()

    loop(1, N, get_fk)
    for p in range(N // 2):
        cols = slice(128 * p, 128 * p + 128)
        a = fkr[2 * p]
        b = fkr[2 * p + 1]
        dk_ref[:, cols] = jnp.concatenate([a[:, :HEAD], b[:, :HEAD]], axis=1)
        dv_ref[:, cols] = jnp.concatenate([a[:, HEAD:], b[:, HEAD:]], axis=1)

    def get_z(d):
        t = lax.rem(z + d, 8)
        remote(zs.at[0], zr.at[t], z_s.at[t], z_rs.at[t], zpeer(t)).wait_recv()

    loop(1, 8, get_z)
    zr[z] = zs[zh]
    whole = wsum[zh]

    def add_z(d, total):
        return total + zr[lax.rem(z + d, 8)].astype(F32)

    dw_ref[...] = lax.fori_loop(1, 8, add_z, whole)

    wa.wait_send()
    do_copy.wait_send()

    def drain(d):
        j = rot(d)
        remote(kvs.at[j], kvo.at[PAD + i0], kv_s.at[j], kv_r.at[i0], peer(j)).wait_send()
        remote(w4.at[i0, :, core], w4.at[i0, :, core], wb_s.at[j], wb_r.at[i0], peer(j)).wait_send()
        remote(qts.at[j], qtr.at[i0], qt_s.at[j], qt_r.at[i0], peer(j)).wait_send()
        remote(gts.at[j], gtr.at[i0], gt_s.at[j], gt_r.at[i0], peer(j)).wait_send()
        remote(dqs.at[j], dqr.at[i0], dq_s.at[j], dq_rs.at[i0], peer(j)).wait_send()
        remote(fks.at[j], fkr.at[i0], fk_s.at[j], fk_rs.at[i0], peer(j)).wait_send()

    loop(1, N, drain)

    def drain_all(j):
        remote(kvo.at[PAD + j], p2.at[1 + j], p2_s.at[j], p2_r.at[j], far).wait_send()
        remote(kvo.at[PAD + j], p1.at[1 + j], p1_s.at[j], p1_r.at[j], sib).wait_send()
        remote(w4.at[j, :, core], w4.at[j, :, core], wc_s.at[j], wc_r.at[j], sib).wait_send()
        remote(d1s.at[j], d1r.at[j], d1_s.at[j], d1_rs.at[j], sib).wait_send()

        @pl.when(jnp.logical_or(zh == 1, j > 0))
        def _():
            remote(d2s.at[j], d2r.at[j], d2_s.at[j], d2_rs.at[j], far).wait_send()


        @pl.when(jnp.logical_not(jnp.logical_and(j == i0, core == half)))
        def _():
            remote(ats.at[j], atr.at[0, 0], at_s.at[j], at_rs.at[0, 0], sib).wait_send()

    loop(0, N, drain_all)

    def drain_w(h):
        head = 2 * h + core
        remote(dws.at[h, :, 1 - core], dwr.at[i0], dw_s.at[h, 1 - core], dw_rs.at[i0], sib).wait_send()

        @pl.when(head != i0)
        def _():
            remote(dws.at[h, :, core], dwr.at[i0], dw_s.at[h, core], dw_rs.at[i0], peer(head)).wait_send()

    loop(0, 8, drain_w)

    def drain_z(d):
        t = lax.rem(z + d, 8)
        remote(zs.at[lax.div(t, 4)], zr.at[z], z_s.at[t], z_rs.at[z], zpeer(t)).wait_send()

    loop(1, 8, drain_z)
    for device, rr in others:
        remote(sumkv.at[r], sumkv.at[r], sm_s.at[rr], sm_r.at[r], device).wait_send()
        remote(accsum.at[pl.ds(16 * rr, 16)], sgr.at[r], sg_s.at[rr], sg_rs.at[r], device).wait_send()


def on_device(queries, keys, values, d_out, out_weight, bar_lengths, summary_pos):
    vm = pltpu.VMEM
    dma = pltpu.SemaphoreType.DMA
    blocks = lambda n, kind=BF: vm((n, BAR, BAR), kind)
    flat = vm((BAR, WIDTH), BF)
    scratch = [
        flat, flat, flat, blocks(N), blocks(PAD + N), blocks(1 + N), blocks(1 + N),
        blocks(PAD + N), blocks(1 + N), blocks(1 + N),
        vm((N, HEAD, BAR), BF), vm((N, HEAD, BAR), BF), vm((N, HEAD, BAR), BF), vm((N, HEAD, BAR), BF),
        vm((N, 2, 2, 16, WIDTH), BF), vm((2, BAR, WIDTH), BF),
        vm((16, BAR), F32), vm((4, 16, BAR), BF), vm((BAR, BAR), BF),
        vm((256, BAR), BF), vm((NKEYS, BAR), F32), vm((NKEYS, 256), BF), vm((NKEYS, BAR), BF), vm((N, NKEYS, BAR), F32),
        vm((NKEYS, BAR), BF), vm((BAR, NKEYS), BF),
        blocks(PAD + N, F32), vm((64, BAR), F32),
        blocks(N), blocks(N), blocks(N), blocks(N), blocks(4, F32), vm((4, 16, BAR), F32),
        blocks(N), blocks(N),
        vm((N, HEAD, BAR), BF), vm((N, HEAD, BAR), BF),
        vm((N, HEAD, BAR), BF), vm((2, 8, HEAD, BAR), BF),
        vm((8, 2, 2, 16, WIDTH), BF), vm((N, 2, 16, WIDTH), BF),
        vm((2, 16, WIDTH), F32), vm((2, 16, WIDTH), BF), vm((8, 16, WIDTH), BF),
    ]
    sems = [(5,)] + [(N,)] * 6 + [(1,)] * 2 + [(N,)] * 4 + [(1,)] * 2 + [(N,)] * 4 + [(4,)] * 2
    sems += [(N,)] * 4 + [(4,)] * 2 + [(N,)] * 4 + [(N,), (2, 8), (8, 2), (N,), (8,), (8,)]
    scratch += [dma(shape) for shape in sems]
    in_vmem = pl.BlockSpec(memory_space=pltpu.VMEM)
    in_smem = pl.BlockSpec(memory_space=pltpu.SMEM)
    rows = jax.ShapeDtypeStruct((BAR, WIDTH), BF)
    d_q, d_k, d_v, d_w = pl.pallas_call(
        kernel,
        out_shape=(rows, rows, rows, jax.ShapeDtypeStruct((16, WIDTH), F32)),
        in_specs=[pl.BlockSpec(memory_space=pltpu.HBM)] * 5 + [in_smem] * 2,
        out_specs=(in_vmem,) * 4,
        scratch_shapes=scratch,
        compiler_params=pltpu.CompilerParams(
            collective_id=0, has_side_effects=True, vmem_limit_bytes=48 * 1024 * 1024
        ),
    )(queries[0, 0], keys[0, 0], values[0, 0], d_out[0, 0], out_weight, bar_lengths, summary_pos)
    return d_q[None, None], d_k[None, None], d_v[None, None], d_w


def solution(mesh):
    spread = P("dp", "ctx", None, None)
    return jax.shard_map(
        on_device,
        mesh=mesh,
        in_specs=(spread,) * 4 + (P("ctx", None), P("dp", None), P("dp", None)),
        out_specs=(spread,) * 3 + (P("ctx", None),),
        check_vma=False,
    )
```

```python
import jax
import jax.numpy as jnp
from jax import lax
from jax.experimental import pallas as pl
from jax.experimental.pallas import tpu as pltpu
from jax.sharding import PartitionSpec as P

N = 16
BAR = 128
HEAD = 64
WIDTH = 1024
PAD = 8
NKEYS = 1280
OWN_STEPS = (1, 2, 3, 4, 6, 8)
BEHIND = 1
AHEAD = 4
LAG_J = 2
LAG = 6
LAG_P = 4
LAG_W = 8
LOW = -1e30
MESH = pl.DeviceIdType.MESH
BF = jnp.bfloat16
F32 = jnp.float32


def remote(src, dst, send, recv, device):
    return pltpu.make_async_remote_copy(
        src_ref=src, dst_ref=dst, send_sem=send, recv_sem=recv, device_id=device, device_id_type=MESH
    )


def loop(low, high, body):
    def step(i, carry):
        body(i)
        return carry

    lax.fori_loop(low, high, step, 0)


def dot_nt(a, b):
    return lax.dot_general(a, b, (((1,), (1,)), ((), ())), preferred_element_type=F32)


def dot(a, b):
    return jnp.dot(a, b, preferred_element_type=F32)


def kernel(
    q_hbm, k_hbm, v_hbm, do_hbm, w_hbm, len_ref, spot_ref,
    dq_ref, dk_ref, dv_ref, dw_ref,
    q_ref, k_ref, v_ref, kvs, kvo, p1, p2, kvot, p1t, p2t, qts, qtr, gts, gtr, w4, do2, sumf, sumkv, sumt,
    b_ref, s_ref, x_ref, pb_ref, ps, cat, catt, acc, accsum, d1s, d1r, d2s, d2r, d2f, sgr,
    fks, fkr, dqs, dqr, ats, atr, dws, dwr, wsum, zs, zr,
    in_s, kv_s, kv_r, p1_s, p1_r, p2_s, p2_r, wa_s, wa_r, wb_s, wb_r, wc_s, wc_r, do_s, do_r,
    qt_s, qt_r, gt_s, gt_r, sm_s, sm_r, d1_s, d1_rs, d2_s, d2_rs, sg_s, sg_rs, fk_s, fk_rs,
    dq_s, dq_rs, at_s, at_rs, dw_s, dw_rs, z_s, z_rs,
):
    dp = lax.axis_index("dp")
    ctx = lax.axis_index("ctx")
    i0 = lax.div(ctx, 4)
    r = lax.rem(ctx, 4)
    zh = lax.div(r, 2)
    core = lax.rem(r, 2)
    z = zh * 4 + dp
    odd = core == 1
    even = core == 0
    me = (dp, ctx)
    sib = (dp, 4 * i0 + 2 * zh + (1 - core))
    far = (dp, 4 * i0 + 2 * (1 - zh) + core)
    diag = (dp, 4 * i0 + 2 * (1 - zh) + (1 - core))

    def peer(j):
        return (dp, 4 * j + r)

    def near(j, c):
        return (dp, 4 * j + 2 * zh + c)

    def zpeer(t):
        return (lax.rem(t, 4), 4 * i0 + 2 * lax.div(t, 4) + core)

    def rot(d):
        return lax.rem(i0 + d, N)

    loads = [
        pltpu.make_async_copy(k_hbm, k_ref, in_s.at[0]),
        pltpu.make_async_copy(v_hbm, v_ref, in_s.at[1]),
        pltpu.make_async_copy(w_hbm, w4.at[i0, zh, core], in_s.at[2]),
        pltpu.make_async_copy(do_hbm, do2.at[core], in_s.at[3]),
        pltpu.make_async_copy(q_hbm, q_ref, in_s.at[4]),
    ]
    for load in loads:
        load.start()

    barrier = pltpu.get_barrier_semaphore()

    def greet(device):
        pl.semaphore_signal(barrier, inc=1, device_id=device, device_id_type=MESH)

    loop(0, N, lambda d: greet(near(rot(d), 1 - core)))
    loop(1, N, lambda d: greet(peer(rot(d))))
    loop(1, 8, lambda d: greet(zpeer(lax.rem(z + d, 8))))
    greet(diag)

    loads[0].wait()
    loads[1].wait()
    for p in range(N // 2):
        cols = slice(128 * p, 128 * p + 128)
        kk = k_ref[:, cols]
        vv = v_ref[:, cols]
        kvs[2 * p] = jnp.concatenate([kk[:, :HEAD], vv[:, :HEAD]], axis=1)
        kvs[2 * p + 1] = jnp.concatenate([kk[:, HEAD:], vv[:, HEAD:]], axis=1)
    kvo[PAD + i0] = kvs[i0]
    loads[2].wait()
    loads[3].wait()
    loads[4].wait()
    for p in range(N // 2):
        qq = (q_ref[:, 128 * p : 128 * p + 128].astype(F32) * 0.125).astype(BF)
        qts[pl.ds(2 * p, 2)] = qq.T.reshape(2, HEAD, BAR)
    qtr[i0] = qts[i0]
    zero = jnp.zeros((BAR, BAR), BF)
    for n in range(PAD):
        kvo[n] = zero
        kvot[n] = zero
    p1[0] = zero
    p1t[0] = zero
    p2[0] = zero
    p2t[0] = zero
    cat[pl.ds(0, 128), :] = zero
    x_ref[pl.ds(0, 128), :] = jnp.zeros((128, 256), BF)
    acc[...] = jnp.zeros(acc.shape, F32)
    accsum[...] = jnp.zeros(accsum.shape, F32)
    wsum[...] = jnp.zeros(wsum.shape, F32)
    pb_ref[pl.ds(0, 128), :] = zero
    pl.semaphore_wait(barrier, 39)

    wa = remote(w4.at[i0, zh, core], w4.at[i0, zh, core], wa_s.at[0], wa_r.at[0], far)
    wa.start()

    def send_kv(d):
        j = rot(d)
        remote(kvs.at[j], kvo.at[PAD + i0], kv_s.at[j], kv_r.at[i0], peer(j)).start()

    loop(1, N, send_kv)

    def send_q(d):
        j = rot(d)
        remote(qts.at[j], qtr.at[i0], qt_s.at[j], qt_r.at[i0], peer(j)).start()

    loop(1, N, send_q)
    do_copy = remote(do2.at[core], do2.at[core], do_s.at[0], do_r.at[0], sib)
    do_copy.start()
    remote(w4.at[i0, 1 - zh, core], w4.at[i0, 1 - zh, core], wa_s.at[0], wa_r.at[0], far).wait_recv()

    step_u = 1 + 3 * core
    step_v = 4 - 3 * core
    pos_u = lax.rem(lax.div(i0, step_u), 4)
    pos_v = lax.rem(lax.div(i0, step_v), 4)

    def cell(du, dv):
        return lax.rem(pos_u + du, 4) * step_u + lax.rem(pos_v + dv, 4) * step_v

    def send_w(j, to, key):
        at = w4.at[j, :, core]
        remote(at, at, wb_s.at[key], wb_r.at[j], peer(to)).start()

    for du in (1, 3, 2):
        send_w(i0, cell(du, 0), cell(du, 0))

    row = lax.broadcasted_iota(jnp.int32, (BAR, BAR), 0)
    col = lax.broadcasted_iota(jnp.int32, (BAR, BAR), 1)

    def pass_on(d):
        j = lax.rem(i0 - d + N, N)

        @pl.when(d > 0)
        def _():
            remote(kvs.at[j], kvo.at[PAD + j], kv_s.at[j], kv_r.at[j], peer(j)).wait_recv()

        remote(kvo.at[PAD + j], p2.at[1 + j], p2_s.at[j], p2_r.at[j], far).start()

        @pl.when(even)
        def _():
            remote(kvo.at[PAD + j], p1.at[1 + j], p1_s.at[j], p1_r.at[j], sib).start()

        block = kvo[PAD + j]
        kvot[PAD + j] = block.T
        spot = spot_ref[0, 4 * j + r]
        picked = jnp.where(row == spot, block.astype(F32), 0.0)
        sumf[pl.ds(j, 1), :] = jnp.sum(picked, axis=0, keepdims=True)

    loop(0, N, pass_on)
    for du in (0, 1, 3, 2):
        j = cell(du, 0)
        if du > 0:
            remote(w4.at[j, :, core], w4.at[j, :, core], wb_s.at[j], wb_r.at[j], peer(j)).wait_recv()
        for dv in (1, 3, 2):
            send_w(j, cell(0, dv), cell(du, dv))
        remote(w4.at[j, :, core], w4.at[j, :, core], wc_s.at[j], wc_r.at[j], sib).start()
    sumkv[r] = sumf[...].astype(BF)
    r_sib = 2 * zh + (1 - core)
    r_far = 2 * (1 - zh) + core
    r_diag = 2 * (1 - zh) + (1 - core)
    others = ((sib, r_sib), (far, r_far), (diag, r_diag))
    for device, rr in others:
        remote(sumkv.at[r], sumkv.at[r], sm_s.at[rr], sm_r.at[r], device).start()

    def pass_w(j, own):
        if not own:
            remote(w4.at[j, :, core], w4.at[j, :, core], wb_s.at[j], wb_r.at[j], peer(j)).wait_recv()
        remote(w4.at[j, :, core], w4.at[j, :, core], wc_s.at[j], wc_r.at[j], sib).start()

    for dv in (1, 3, 2):
        for du in (0, 1, 3, 2):
            pass_w(cell(du, dv), False)

    def project_back():
        for c in range(4):
            line = lax.rem(lax.div(i0, 4) + c, 4)
            for n in range(4):
                j = 4 * line + n
                remote(w4.at[j, :, 1 - core], w4.at[j, :, 1 - core], wc_s.at[j], wc_r.at[j], sib).wait_recv()
            rows = w4[pl.ds(4 * line, 4)].reshape(256, WIDTH)
            gts[pl.ds(4 * line, 4)] = dot_nt(rows, do2[core]).astype(BF).reshape(4, HEAD, BAR)
            for n in range(4):
                h = 4 * line + lax.rem(i0 + n, 4)

                @pl.when(i0 != h)
                def _():
                    remote(gts.at[h], gtr.at[i0], gt_s.at[h], gt_r.at[i0], peer(h)).start()

        gtr[i0] = gts[i0]

    project_back()

    for device, rr in others:
        remote(sumkv.at[rr], sumkv.at[rr], sm_s.at[rr], sm_r.at[rr], device).wait_recv()
    cat[pl.ds(0, 64), :] = sumkv[...].reshape(64, BAR)
    catt[:, pl.ds(0, 128)] = cat[pl.ds(0, 128), :].T

    def behind(t):
        return lax.rem(i0 - t + N, N)

    def take_far(t):
        j = behind(t)
        remote(kvo.at[PAD + j], p2.at[1 + j], p2_s.at[j], p2_r.at[j], far).wait_recv()

        @pl.when(odd)
        def _():
            remote(p2.at[1 + j], p1.at[1 + j], p1_s.at[j], p1_r.at[j], sib).start()

        p2t[1 + j] = p2[1 + j].T

    def take_near(t):
        j = behind(t)
        remote(kvo.at[PAD + j], p1.at[1 + j], p1_s.at[j], p1_r.at[j], sib).wait_recv()
        p1t[1 + j] = p1[1 + j].T

    loop(0, AHEAD, take_far)
    loop(0, AHEAD - 2, take_near)

    lag1 = jnp.where(r < 1, 1, 0)
    lag2 = jnp.where(r < 2, 1, 0)
    srow = lax.broadcasted_iota(jnp.int32, (64, BAR), 0)
    sbar = 4 * lax.rem(srow, 16) + lax.div(srow, 16)
    left = col < HEAD

    half = lax.rem(i0, 2)
    slot = lax.div(i0, 2)

    def send_far(i):
        @pl.when(jnp.logical_or(zh == 1, i > 0))
        def _():
            remote(d2s.at[i], d2r.at[i], d2_s.at[i], d2_rs.at[i], far).start()

    def join(i):
        @pl.when(odd)
        def _():
            remote(d1s.at[i], d1r.at[i], d1_s.at[i], d1_rs.at[i], sib).wait_recv()
            d2s[i] = (d2f[lax.rem(i, 4)] + d1r[i].astype(F32)).astype(BF)
            send_far(i)

    def take_terms(t):
        at = behind(t)

        @pl.when(jnp.logical_or(zh == 0, at > 0))
        def _():
            remote(d2s.at[at], d2r.at[at], d2_s.at[at], d2_rs.at[at], far).wait_recv()
            acc[PAD + at - zh] += d2r[at].astype(F32)

        @pl.when(even)
        def _():
            remote(d1s.at[at], d1r.at[at], d1_s.at[at], d1_rs.at[at], sib).wait_recv()
            acc[PAD + at] += d1r[at].astype(F32)

    def project(t):
        head = rot(t)

        @pl.when(lax.rem(head, 2) == core)
        def _():
            at = lax.div(head, 2)
            for c in range(2):
                @pl.when(jnp.logical_not(jnp.logical_and(t == 0, core == c)))
                def _():
                    remote(ats.at[0], atr.at[c, at], at_s.at[0], at_rs.at[c, at], sib).wait_recv()

            lhs = jnp.concatenate([atr[0, at], atr[1, at]], axis=1)
            part = dot(lhs, do2[...].reshape(256, WIDTH)).astype(BF)
            dws[at] = part.reshape(2, 2, 16, WIDTH)
            remote(
                dws.at[at, :, 1 - core], dwr.at[i0], dw_s.at[at, 1 - core], dw_rs.at[i0], near(head, 1 - core)
            ).start()

            @pl.when(t > 0)
            def _():
                remote(dws.at[at, :, core], dwr.at[i0], dw_s.at[at, core], dw_rs.at[i0], peer(head)).start()

            @pl.when(t == 0)
            def _():
                dwr[i0] = dws[at, :, core]

    def take_dw(t):
        j = behind(t)

        @pl.when(jnp.logical_not(jnp.logical_and(t == 0, core == half)))
        def _():
            remote(dws.at[0, :, 0], dwr.at[j], dw_s.at[0, 0], dw_rs.at[j], sib).wait_recv()

        wsum[...] += dwr[j].astype(F32)

    remote(do2.at[1 - core], do2.at[1 - core], do_s.at[0], do_r.at[0], sib).wait_recv()

    def gather(i, steps, lens=None):
        bar = 4 * i + r
        blocks = [(kvo, kvot, PAD + i, 0), (p1, p1t, 1 + i - lag1, 1), (p2, p2t, 1 + i - lag2, 2)]
        blocks += [(kvo, kvot, PAD + i - m, 4 * m) for m in steps]
        for n, (src, srct, at, offset) in enumerate(blocks):
            cat[pl.ds(128 * n + 128, 128), :] = src[at]
            catt[:, pl.ds(128 * n + 128, 128)] = srct[at]
            if lens is not None:
                source = bar - offset
                length = len_ref[0, jnp.maximum(source, 0)]
                lens.append(jnp.where(source >= 0, length, 0))
        spans = [(128 * n + 128, 128) for n in range(len(blocks))] + [(0, 64)]
        return blocks, spans, 128 * len(blocks) + 128

    nothing = jnp.zeros((HEAD, BAR), BF)

    def forward(i, steps):
        bar = 4 * i + r
        lens = []
        blocks, spans, size_all = gather(i, steps, lens)
        rhs = jnp.concatenate([qtr[i], nothing], axis=0)
        s_ref[pl.ds(0, size_all), :] = dot(cat[pl.ds(0, size_all), :], rhs)
        top = jnp.full((8, BAR), LOW, F32)
        for n, (at, size) in enumerate(spans):
            s = s_ref[pl.ds(at, size), :]
            if n == 0:
                keep = (row <= col) & (row < lens[0])
            elif n < len(blocks):
                keep = row < lens[n]
            else:
                keep = sbar < bar
            s = jnp.where(keep, s, LOW)
            s_ref[pl.ds(at, size), :] = s
            top = jnp.maximum(top, jnp.max(s.reshape(size // 8, 8, BAR), axis=0))
        top = jnp.max(top, axis=0, keepdims=True)
        total = jnp.zeros((8, BAR), F32)
        for at, size in spans:
            e = jnp.exp(s_ref[pl.ds(at, size), :] - top)
            s_ref[pl.ds(at, size), :] = e
            total = total + jnp.sum(e.reshape(size // 8, 8, BAR), axis=0)
        inv = 1.0 / jnp.sum(total, axis=0, keepdims=True)
        for at, size in spans:
            prob = s_ref[pl.ds(at, size), :] * inv
            ps[i, pl.ds(at, size), :] = prob
            pb_ref[pl.ds(at, size), :] = prob.astype(BF)
        out = dot(catt[HEAD:BAR, pl.ds(0, size_all)], pb_ref[pl.ds(0, size_all), :])
        ats[i] = out.astype(BF)

    def backward(i, steps):
        blocks, spans, size_all = gather(i, steps)
        rhs = jnp.concatenate([nothing, gtr[i]], axis=0)
        s_ref[pl.ds(0, size_all), :] = dot(cat[pl.ds(0, size_all), :], rhs)
        delta = jnp.zeros((8, BAR), F32)
        for at, size in spans:
            pb = ps[i, pl.ds(at, size), :].astype(BF)
            x_ref[pl.ds(at, size), 128:256] = pb
            term = pb.astype(F32) * s_ref[pl.ds(at, size), :]
            delta = delta + jnp.sum(term.reshape(size // 8, 8, BAR), axis=0)
        delta = jnp.sum(delta, axis=0, keepdims=True)
        for at, size in spans:
            ds = ps[i, pl.ds(at, size), :] * (s_ref[pl.ds(at, size), :] - delta)
            x_ref[pl.ds(at, size), 0:128] = ds.astype(BF)
        qg = jnp.concatenate([qtr[i], gtr[i]], axis=0).T
        none = jnp.zeros_like(qg)
        b_ref[pl.ds(0, 128), :] = jnp.where(left, qg, none)
        b_ref[pl.ds(128, 128), :] = jnp.where(left, none, qg)
        rhs = b_ref[...]
        for n in (1, 2, 0) + tuple(range(3, len(blocks))):
            term = dot(x_ref[pl.ds(128 * n + 128, 128), :], rhs)
            at = blocks[n][2]
            if n == 1:
                d1s[i] = term.astype(BF)
                remote(d1s.at[i], d1r.at[i], d1_s.at[i], d1_rs.at[i], sib).start()
            elif n == 2:
                d2f[lax.rem(i, 4)] = term

                @pl.when(even)
                def _():
                    d2s[i] = term.astype(BF)
                    send_far(i)
            else:
                acc[at] += term
        accsum[...] += dot(x_ref[pl.ds(0, 64), :], rhs)
        out = dot(catt[0:HEAD, pl.ds(0, size_all)], x_ref[pl.ds(0, size_all), 0:128])
        dqs[i] = (out * 0.125).astype(BF)

    def by_reach(i, work):
        @pl.when(i >= 8)
        def _():
            work(i, OWN_STEPS)

        @pl.when(jnp.logical_and(i >= 4, i < 8))
        def _():
            work(i, OWN_STEPS[:5])

        @pl.when(i < 4)
        def _():
            work(i, OWN_STEPS[:3])

    def first(t):
        i = behind(t)

        @pl.when(t + AHEAD < N)
        def _():
            take_far(t + AHEAD)

        @pl.when(t + AHEAD - 2 < N)
        def _():
            take_near(t + AHEAD - 2)

        @pl.when(i != i0)
        def _():
            remote(qts.at[i], qtr.at[i], qt_s.at[i], qt_r.at[i], peer(i)).wait_recv()

        by_reach(i, forward)
        here = jnp.logical_and(i == i0, core == half)

        @pl.when(jnp.logical_not(here))
        def _():
            remote(ats.at[i], atr.at[core, slot], at_s.at[i], at_rs.at[core, slot], near(i, half)).start()

        @pl.when(here)
        def _():
            atr[core, slot] = ats[i]

    def second(t):
        i = behind(t)

        @pl.when(i != i0)
        def _():
            remote(gts.at[i], gtr.at[i], gt_s.at[i], gt_r.at[i], peer(i)).wait_recv()

        by_reach(i, backward)

        @pl.when(i != i0)
        def _():
            remote(dqs.at[i], dqr.at[i0], dq_s.at[i], dq_rs.at[i0], peer(i)).start()

        @pl.when(i == i0)
        def _():
            dqr[i] = dqs[i]

    def send_z(d):
        t = lax.rem(z + d, 8)
        remote(zs.at[lax.div(t, 4)], zr.at[z], z_s.at[t], z_rs.at[z], zpeer(t)).start()

    def share_sum():
        zs[...] = wsum[...].astype(BF)
        loop(1, 8, send_z)

    def step(t):
        @pl.when(t < N)
        def _():
            first(t)

        @pl.when(jnp.logical_and(t >= LAG_P, t < N + LAG_P))
        def _():
            project(t - LAG_P)

        @pl.when(jnp.logical_and(t >= LAG_W, t < N + LAG_W))
        def _():
            take_dw(t - LAG_W)

        if LAG_W < BEHIND:
            @pl.when(t == N + LAG_W)
            def _():
                share_sum()

        @pl.when(t >= BEHIND)
        def _():
            second(t - BEHIND)

        @pl.when(t >= BEHIND + LAG_J)
        def _():
            join(behind(t - BEHIND - LAG_J))

        @pl.when(t >= BEHIND + LAG)
        def _():
            take_terms(t - BEHIND - LAG)

    loop(0, N + BEHIND, step)
    loop(N - LAG_J, N, lambda t: join(behind(t)))
    for device, rr in others:
        remote(accsum.at[pl.ds(16 * rr, 16)], sgr.at[r], sg_s.at[rr], sg_rs.at[r], device).start()
    loop(min(N, N + BEHIND - LAG_P), N, project)
    if LAG_W >= BEHIND:
        loop(N + BEHIND - LAG_W, N, take_dw)
        share_sum()
    loop(N - LAG, N, take_terms)

    for device, rr in others:
        remote(sgr.at[rr], sgr.at[rr], sg_s.at[rr], sg_rs.at[rr], device).wait_recv()
    sgr[r] = accsum[pl.ds(16 * r, 16), :]
    sumf[...] = sgr[0] + sgr[1] + sgr[2] + sgr[3]

    def finish(d):
        j = rot(d)
        spot = spot_ref[0, 4 * j + r]
        extra = jnp.where(row == spot, sumf[pl.ds(j, 1), :], 0.0)
        fks[j] = (acc[PAD + j] + extra).astype(BF)

        @pl.when(d > 0)
        def _():
            remote(fks.at[j], fkr.at[i0], fk_s.at[j], fk_rs.at[i0], peer(j)).start()

    loop(0, N, finish)
    fkr[i0] = fks[i0]

    def get_dq(d):
        j = rot(d)
        remote(dqs.at[j], dqr.at[j], dq_s.at[j], dq_rs.at[j], peer(j)).wait_recv()

    loop(1, N, get_dq)
    for p in range(N // 2):
        dq_ref[:, 128 * p : 128 * p + 128] = dqr[2 * p : 2 * p + 2].reshape(128, 128).T

    def get_fk(d):
        j = rot(d)
        remote(fks.at[j], fkr.at[j], fk_s.at[j], fk_rs.at[j], peer(j)).wait_recv()

    loop(1, N, get_fk)
    for p in range(N // 2):
        cols = slice(128 * p, 128 * p + 128)
        a = fkr[2 * p]
        b = fkr[2 * p + 1]
        dk_ref[:, cols] = jnp.concatenate([a[:, :HEAD], b[:, :HEAD]], axis=1)
        dv_ref[:, cols] = jnp.concatenate([a[:, HEAD:], b[:, HEAD:]], axis=1)

    def get_z(d):
        t = lax.rem(z + d, 8)
        remote(zs.at[0], zr.at[t], z_s.at[t], z_rs.at[t], zpeer(t)).wait_recv()

    loop(1, 8, get_z)
    zr[z] = zs[zh]
    whole = wsum[zh]

    def add_z(d, total):
        return total + zr[lax.rem(z + d, 8)].astype(F32)

    dw_ref[...] = lax.fori_loop(1, 8, add_z, whole)

    wa.wait_send()
    do_copy.wait_send()

    def drain(d):
        j = rot(d)
        remote(kvs.at[j], kvo.at[PAD + i0], kv_s.at[j], kv_r.at[i0], peer(j)).wait_send()
        remote(w4.at[i0, :, core], w4.at[i0, :, core], wb_s.at[j], wb_r.at[i0], peer(j)).wait_send()
        remote(qts.at[j], qtr.at[i0], qt_s.at[j], qt_r.at[i0], peer(j)).wait_send()
        remote(gts.at[j], gtr.at[i0], gt_s.at[j], gt_r.at[i0], peer(j)).wait_send()
        remote(dqs.at[j], dqr.at[i0], dq_s.at[j], dq_rs.at[i0], peer(j)).wait_send()
        remote(fks.at[j], fkr.at[i0], fk_s.at[j], fk_rs.at[i0], peer(j)).wait_send()

    loop(1, N, drain)

    def drain_all(j):
        remote(kvo.at[PAD + j], p2.at[1 + j], p2_s.at[j], p2_r.at[j], far).wait_send()
        remote(kvo.at[PAD + j], p1.at[1 + j], p1_s.at[j], p1_r.at[j], sib).wait_send()
        remote(w4.at[j, :, core], w4.at[j, :, core], wc_s.at[j], wc_r.at[j], sib).wait_send()
        remote(d1s.at[j], d1r.at[j], d1_s.at[j], d1_rs.at[j], sib).wait_send()

        @pl.when(jnp.logical_or(zh == 1, j > 0))
        def _():
            remote(d2s.at[j], d2r.at[j], d2_s.at[j], d2_rs.at[j], far).wait_send()


        @pl.when(jnp.logical_not(jnp.logical_and(j == i0, core == half)))
        def _():
            remote(ats.at[j], atr.at[0, 0], at_s.at[j], at_rs.at[0, 0], sib).wait_send()

    loop(0, N, drain_all)

    def drain_w(h):
        head = 2 * h + core
        remote(dws.at[h, :, 1 - core], dwr.at[i0], dw_s.at[h, 1 - core], dw_rs.at[i0], sib).wait_send()

        @pl.when(head != i0)
        def _():
            remote(dws.at[h, :, core], dwr.at[i0], dw_s.at[h, core], dw_rs.at[i0], peer(head)).wait_send()

    loop(0, 8, drain_w)

    def drain_z(d):
        t = lax.rem(z + d, 8)
        remote(zs.at[lax.div(t, 4)], zr.at[z], z_s.at[t], z_rs.at[z], zpeer(t)).wait_send()

    loop(1, 8, drain_z)
    for device, rr in others:
        remote(sumkv.at[r], sumkv.at[r], sm_s.at[rr], sm_r.at[r], device).wait_send()
        remote(accsum.at[pl.ds(16 * rr, 16)], sgr.at[r], sg_s.at[rr], sg_rs.at[r], device).wait_send()


def on_device(queries, keys, values, d_out, out_weight, bar_lengths, summary_pos):
    vm = pltpu.VMEM
    dma = pltpu.SemaphoreType.DMA
    blocks = lambda n, kind=BF: vm((n, BAR, BAR), kind)
    flat = vm((BAR, WIDTH), BF)
    scratch = [
        flat, flat, flat, blocks(N), blocks(PAD + N), blocks(1 + N), blocks(1 + N),
        blocks(PAD + N), blocks(1 + N), blocks(1 + N),
        vm((N, HEAD, BAR), BF), vm((N, HEAD, BAR), BF), vm((N, HEAD, BAR), BF), vm((N, HEAD, BAR), BF),
        vm((N, 2, 2, 16, WIDTH), BF), vm((2, BAR, WIDTH), BF),
        vm((16, BAR), F32), vm((4, 16, BAR), BF), vm((BAR, BAR), BF),
        vm((256, BAR), BF), vm((NKEYS, BAR), F32), vm((NKEYS, 256), BF), vm((NKEYS, BAR), BF), vm((N, NKEYS, BAR), F32),
        vm((NKEYS, BAR), BF), vm((BAR, NKEYS), BF),
        blocks(PAD + N, F32), vm((64, BAR), F32),
        blocks(N), blocks(N), blocks(N), blocks(N), blocks(4, F32), vm((4, 16, BAR), F32),
        blocks(N), blocks(N),
        vm((N, HEAD, BAR), BF), vm((N, HEAD, BAR), BF),
        vm((N, HEAD, BAR), BF), vm((2, 8, HEAD, BAR), BF),
        vm((8, 2, 2, 16, WIDTH), BF), vm((N, 2, 16, WIDTH), BF),
        vm((2, 16, WIDTH), F32), vm((2, 16, WIDTH), BF), vm((8, 16, WIDTH), BF),
    ]
    sems = [(5,)] + [(N,)] * 6 + [(1,)] * 2 + [(N,)] * 4 + [(1,)] * 2 + [(N,)] * 4 + [(4,)] * 2
    sems += [(N,)] * 4 + [(4,)] * 2 + [(N,)] * 4 + [(N,), (2, 8), (8, 2), (N,), (8,), (8,)]
    scratch += [dma(shape) for shape in sems]
    in_vmem = pl.BlockSpec(memory_space=pltpu.VMEM)
    in_smem = pl.BlockSpec(memory_space=pltpu.SMEM)
    rows = jax.ShapeDtypeStruct((BAR, WIDTH), BF)
    d_q, d_k, d_v, d_w = pl.pallas_call(
        kernel,
        out_shape=(rows, rows, rows, jax.ShapeDtypeStruct((16, WIDTH), F32)),
        in_specs=[pl.BlockSpec(memory_space=pltpu.HBM)] * 5 + [in_smem] * 2,
        out_specs=(in_vmem,) * 4,
        scratch_shapes=scratch,
        compiler_params=pltpu.CompilerParams(
            collective_id=0, has_side_effects=True, vmem_limit_bytes=48 * 1024 * 1024
        ),
    )(queries[0, 0], keys[0, 0], values[0, 0], d_out[0, 0], out_weight, bar_lengths, summary_pos)
    return d_q[None, None], d_k[None, None], d_v[None, None], d_w


def solution(mesh):
    spread = P("dp", "ctx", None, None)
    return jax.shard_map(
        on_device,
        mesh=mesh,
        in_specs=(spread,) * 4 + (P("ctx", None), P("dp", None), P("dp", None)),
        out_specs=(spread,) * 3 + (P("ctx", None),),
        check_vma=False,
    )
```
